256 devices in a mesh: ctx: 64 (over y, z, x_lo), head: 4 (over x_hi, core).
Axes of the slice: x: 4 (x_hi: 2, x_lo: 2; x = x_hi * 2 + x_lo), y: 4, z: 8, core: 2. Of those that a mesh axis runs over, the one named last changes fastest.
Arguments:
- queries: bfloat16 [512, 64, 128], P('ctx', 'head'), may hold values from -120 to 120
- cache_keys: bfloat16 [16384, 4, 128], P('ctx', 'head'), may hold values from -5 to 5
- stored_cache_values: bfloat16 [16384, 4, 128], P('ctx', 'head'), may hold values from -5 to 5
- turn_keys: bfloat16 [512, 4, 128], P('ctx', 'head'), may hold values from -5 to 5
- turn_values: bfloat16 [512, 4, 128], P('ctx', 'head'), may hold values from -5 to 5
- block_mask: int32 [4, 128], replicated, may hold values from 0 to 1, as said below
- doc_ids: int32 [512], replicated, may hold values from 0 to 7, never falling along the last dimension, each value on 1 to 256 neighbouring positions
- slot_ids: int32 [128], replicated, may hold values from 0 to 255, as said below
- out_weight: bfloat16 [8192, 16384], P('head', 'ctx'), may hold values from -0.0625 to 0.0625
Outputs:
- layer_out: float32 [512, 16384], P('head', 'ctx')
- append_slot_keys: bfloat16 [1024, 4, 128], P('ctx', 'head')
- append_slot_values: bfloat16 [1024, 4, 128], P('ctx', 'head')
The draws below stay inside these ranges and needn't reach their ends.
Inputs may be any that keep to these rules, and one draw needn't show every extreme that they name: `block_mask`: column 0 and the last two columns are 1 in every row. `slot_ids`: distinct; piece p is kept by ctx index slot_ids[p] // 4 in its slot slot_ids[p] % 4. `doc_ids`: never falling along the new turn.
All inputs are finite; a program needn't handle non-finite values.
Results may differ from the reference program's by a relative error of at most 0.012.
Values may be sent and summed in bfloat16 or wider, within the bound.
A program may use at most 64 MiB of HBM per device.

```python
import math
import jax
import jax.numpy as jnp
import numpy as np
from jax import lax

D = 16384
QUERY_HEADS = 64
KEY_VALUE_HEADS = 4
HEAD_SIZE = 128
BLK = 128
SLOTS = 4
TURN_TOKENS = 512
CACHE_DEV = 256
CACHED_POSITIONS = 16384
QBLK = 4
CBLK = 128
PIECE_TOTAL = 128
PIECE_ROWS = 4
N_CTX = 64


def shared_keys(key):
    return jax.random.truncated_normal(key, -5.0, 5.0, (CACHED_POSITIONS, KEY_VALUE_HEADS, HEAD_SIZE), jnp.float32)


def draw_cache_keys(key, part):
    base = shared_keys(key)
    return base.astype(jnp.bfloat16)


def draw_queries(key, part):
    own_key = jax.random.fold_in(key, 5)
    values = jax.random.truncated_normal(own_key, -5.0, 5.0, (TURN_TOKENS, QUERY_HEADS, HEAD_SIZE), jnp.float32)
    return values.astype(jnp.bfloat16)


def draw_block_mask(key, part):
    key = jax.random.fold_in(key, 7)
    key_a, key_b, key_c, key_d = jax.random.split(key, 4)
    columns = jnp.arange(CBLK, dtype=jnp.int32)[None, :]
    start_one = jax.random.randint(key_a, (QBLK, 1), 0, CBLK)
    start_two = jax.random.randint(key_b, (QBLK, 1), 0, CBLK)
    start = jnp.minimum(start_one, start_two)
    length = jax.random.randint(key_c, (QBLK, 1), 2, 3 + CBLK // 8)
    run_part = (columns >= start) & (columns < start + length)
    sprinkle = jax.random.randint(key_d, (QBLK, CBLK), 0, 8) == 0
    sink_part = columns == 0
    band_part = columns >= CBLK - 2
    return (run_part | sprinkle | sink_part | band_part).astype(jnp.int32)


def draw_slot_ids(key, part):
    key = jax.random.fold_in(key, 9)
    key_a, key_b = jax.random.split(key)
    slots_overall = N_CTX * SLOTS
    picked = jax.random.permutation(key_a, jnp.arange(slots_overall, dtype=jnp.int32))[:PIECE_TOTAL]
    where_max = jax.random.randint(key_b, (), 0, PIECE_TOTAL)
    has_max = jnp.any(picked == slots_overall - 1)
    forced = picked.at[where_max].set(slots_overall - 1)
    return jnp.where(has_max, picked, forced).astype(jnp.int32)


def steps_of(rng, dims, cuts, low, top_value):
    level, own = 1.0, jax.random.fold_in(rng, 6)
    for position, shards_of in cuts:
        steps = jnp.exp(jax.random.uniform(jax.random.fold_in(own, position), (shards_of,), jnp.float32, low / len(cuts), top_value / len(cuts)))
        level = level * jnp.repeat(steps, dims[position] // shards_of).reshape([-1 if axis == position else 1 for axis in range(len(dims))])
    return level


def length_profile(amount, total, limit, skew):
    weights = [(1 << 20) // math.isqrt(rank ** skew) + 1 for rank in range(2, amount + 1)]
    rest, counts = total - limit - (amount - 1), [1] * (amount - 1)
    while rest > 0:
        movable = [i for i in range(amount - 1) if counts[i] < limit]
        mass, remaining = sum([weights[i] for i in movable]), rest
        for i in movable:
            more = min(limit - counts[i], max(1, remaining * weights[i] // mass), rest)
            counts[i] = counts[i] + more
            rest = rest - more
    return np.array([limit] + counts)


def ragged(key, number_of, total, limit, slope):
    if number_of == 2:
        one = jax.random.randint(key, (), max(1, total - limit), min(limit, total - 1) + 1)
        return jnp.stack([one, total - one])
    tallies = jnp.asarray(length_profile(number_of, total, limit, slope), jnp.int32)
    pairs = (number_of - 1) // 2
    source_of, sink = tallies[1:1 + 2 * pairs:2], tallies[2:2 + 2 * pairs:2]
    margin = jnp.minimum(source_of - 1, limit - sink)
    shifted = jax.random.randint(jax.random.fold_in(key, 1), (pairs,), 0, 1 << 20) % (margin + 1)
    tallies = tallies.at[1:1 + 2 * pairs:2].set(source_of - shifted).at[2:2 + 2 * pairs:2].set(sink + shifted)
    return tallies[jax.random.permutation(jax.random.fold_in(key, 2), number_of)]


def bell_draw(key, extent, scale, limit, pieces=(), kind=jnp.bfloat16):
    values = scale * jax.random.normal(key, extent, jnp.float32)
    if pieces:
        values = values * steps_of(key, extent, pieces, -0.22, 0.18)
    return jnp.clip(values, -limit, limit).astype(kind)


def setup_inputs(seed: int = 0) -> dict:
    key_list = jax.random.split(jax.random.key(seed), 10)
    queries = draw_queries(jax.random.fold_in(key_list[9], 71), 0)
    cache_keys = draw_cache_keys(jax.random.fold_in(key_list[9], 71), 0)
    stored_cache_values = bell_draw(key_list[2], (CACHED_POSITIONS, KEY_VALUE_HEADS, HEAD_SIZE), 1.0, 5.0, ((0, 64), (1, 4)))
    turn_keys = bell_draw(key_list[3], (TURN_TOKENS, KEY_VALUE_HEADS, HEAD_SIZE), 1.0, 5.0, ((0, 64), (1, 4)))
    turn_values = bell_draw(key_list[4], (TURN_TOKENS, KEY_VALUE_HEADS, HEAD_SIZE), 1.0, 5.0, ((0, 64), (1, 4)))
    block_mask = draw_block_mask(jax.random.fold_in(key_list[9], 71), 0)
    doc_ids = jnp.searchsorted(jnp.cumsum(ragged(key_list[6], TURN_TOKENS // BLK + 4, TURN_TOKENS, 2 * BLK, 0)), jnp.arange(TURN_TOKENS), side="right").astype(jnp.int32)
    slot_ids = draw_slot_ids(jax.random.fold_in(key_list[9], 71), 0)
    out_weight = bell_draw(key_list[8], (QUERY_HEADS * HEAD_SIZE, D), (QUERY_HEADS * HEAD_SIZE) ** -0.5, 0.0625, ((0, 4), (1, 64)))
    return dict(queries=queries, cache_keys=cache_keys, stored_cache_values=stored_cache_values, turn_keys=turn_keys, turn_values=turn_values, block_mask=block_mask, doc_ids=doc_ids, slot_ids=slot_ids, out_weight=out_weight)


NEG_FILL = -1e+30

def attend(query_rows, key_rows, value_rows, allowed):
    row_count = query_rows.shape[0]
    kv_heads = key_rows.shape[1]
    head_width = query_rows.shape[2]
    group_size = query_rows.shape[1] // kv_heads
    grouped = query_rows.reshape(row_count, kv_heads, group_size, head_width).astype(jnp.float32)
    scores = jnp.einsum('nkgd,mkd->nkgm', grouped, key_rows.astype(jnp.float32)) * (1.0 / math.sqrt(head_width))
    mask_four = allowed[:, None, None, :]
    peak_score = lax.optimization_barrier(jnp.max(jnp.where(mask_four, scores, NEG_FILL), axis=-1))
    softmax_terms = jnp.where(mask_four, jnp.exp(scores - peak_score[..., None]), 0.0)
    weight_sum = lax.optimization_barrier(jnp.sum(softmax_terms, axis=-1))
    weights = softmax_terms.astype(jnp.bfloat16)
    output = jnp.einsum('nkgm,mkd->nkgd', weights.astype(jnp.float32), value_rows.astype(jnp.float32))
    return (peak_score, weight_sum, output)

def combine(earlier, later):
    new_peak = jnp.maximum(earlier[0], later[0])
    scale_one = jnp.exp(earlier[0] - new_peak)
    scale_two = jnp.exp(later[0] - new_peak)
    return (new_peak, earlier[1] * scale_one + later[1] * scale_two, earlier[2] * scale_one[..., None] + later[2] * scale_two[..., None])

def reference(queries, cache_keys, stored_cache_values, turn_keys, turn_values, block_mask, doc_ids, slot_ids, out_weight):
    slots_overall = N_CTX * SLOTS
    select = slot_ids[None, :] == jnp.arange(slots_overall, dtype=jnp.int32)[:, None]
    picker_function = select.astype(jnp.bfloat16)
    flattened_width = PIECE_ROWS * KEY_VALUE_HEADS * HEAD_SIZE
    append_slot_keys = jnp.dot(picker_function, turn_keys.reshape(PIECE_TOTAL, flattened_width), preferred_element_type=jnp.float32).astype(jnp.bfloat16).reshape(slots_overall * PIECE_ROWS, KEY_VALUE_HEADS, HEAD_SIZE)
    append_slot_values = jnp.dot(picker_function, turn_values.reshape(PIECE_TOTAL, flattened_width), preferred_element_type=jnp.float32).astype(jnp.bfloat16).reshape(slots_overall * PIECE_ROWS, KEY_VALUE_HEADS, HEAD_SIZE)
    slot_piece = lax.optimization_barrier(jnp.sum(jnp.where(select, jnp.arange(PIECE_TOTAL, dtype=jnp.int32)[None, :], 0), axis=1))
    slot_live = jnp.any(select, axis=1)
    positions = jnp.arange(TURN_TOKENS, dtype=jnp.int32)
    within = jnp.arange(PIECE_ROWS, dtype=jnp.int32)

    def group_step(carried, group_index):
        cache_part_k = lax.dynamic_slice_in_dim(cache_keys, group_index * CACHE_DEV, CACHE_DEV, 0)
        cache_part_v = lax.dynamic_slice_in_dim(stored_cache_values, group_index * CACHE_DEV, CACHE_DEV, 0)
        slot_part_k = lax.dynamic_slice_in_dim(append_slot_keys, group_index * SLOTS * PIECE_ROWS, SLOTS * PIECE_ROWS, 0)
        slot_part_v = lax.dynamic_slice_in_dim(append_slot_values, group_index * SLOTS * PIECE_ROWS, SLOTS * PIECE_ROWS, 0)
        pieces_here = lax.dynamic_slice_in_dim(slot_piece, group_index * SLOTS, SLOTS, 0)
        live_here = lax.dynamic_slice_in_dim(slot_live, group_index * SLOTS, SLOTS, 0)
        new_pos = (pieces_here[:, None] * PIECE_ROWS + within[None, :]).reshape(-1)
        new_live = jnp.repeat(live_here, PIECE_ROWS)
        new_docs = jnp.take(doc_ids, new_pos)
        columns = lax.dynamic_slice_in_dim(block_mask, group_index * (CACHE_DEV // BLK), CACHE_DEV // BLK, 1)
        cache_allowed = jnp.repeat(jnp.repeat(columns, BLK, axis=0), BLK, axis=1) == 1
        new_allowed = new_live[None, :] & (new_pos[None, :] <= positions[:, None]) & (new_docs[None, :] == doc_ids[:, None])
        allowed = jnp.concatenate([cache_allowed, new_allowed], axis=1)
        key_rows = jnp.concatenate([cache_part_k, slot_part_k], axis=0)
        value_rows = jnp.concatenate([cache_part_v, slot_part_v], axis=0)
        return (combine(carried, attend(queries, key_rows, value_rows, allowed)), None)
    reduced_shape = (TURN_TOKENS, KEY_VALUE_HEADS, QUERY_HEADS // KEY_VALUE_HEADS)
    initial = (jnp.full(reduced_shape, NEG_FILL, jnp.float32), jnp.zeros(reduced_shape, jnp.float32), jnp.zeros(reduced_shape + (HEAD_SIZE,), jnp.float32))
    carried, unused = lax.scan(group_step, initial, jnp.arange(N_CTX, dtype=jnp.int32))
    attended = (carried[2] / carried[1][..., None]).astype(jnp.bfloat16).reshape(TURN_TOKENS, QUERY_HEADS * HEAD_SIZE)
    layer_out = jnp.dot(attended, out_weight, preferred_element_type=jnp.float32)
    return (layer_out, append_slot_keys, append_slot_values)
```

```python
import math

import jax
import jax.numpy as jnp
from jax import lax
from jax.experimental import pallas as pl
from jax.experimental.pallas import tpu as pltpu
from jax.sharding import PartitionSpec as P

MESH = pl.DeviceIdType.MESH
F32 = jnp.float32
BF16 = jnp.bfloat16

NY, NZ, NX = 4, 8, 2
NYX = NY * NX
HEAD = 128
KEYS = 256
GROUP = 16
ROWS = 8
NEG = -1e30
FLOOR = -1e29
SCALE = math.log2(math.e) / math.sqrt(HEAD)

YX = [(0, 0), (0, 1), (1, 0), (3, 0), (1, 1), (3, 1), (2, 0), (2, 1)]
PAIRS = [YX[0:2], YX[2:4], YX[4:6], YX[6:8]]


def nt(a, b):
    return lax.dot_general(a, b, (((1,), (1,)), ((), ())), preferred_element_type=F32)


def mm(a, b):
    return jnp.dot(a, b, preferred_element_type=F32)


def iota(shape, dim):
    return lax.broadcasted_iota(jnp.int32, shape, dim)


def kernel(
    q_in, ck_in, cv_in, w_in, tk_ref, tv_ref, doc_ref, slot_ref, mask_ref,
    out_ref, ak_ref, av_ref,
    q_raw, q_send, q_all, k_all, v_all, vt_all, w_all, turn,
    peak, acc, o_send, st_send, o_recv, st_recv, part_a, part_b, terms, h_send, h_recv, x_recv,
    sem_in, sem_q, sem_kv, sem_t, sem_tt, sem_rs, sem_a1, sem_b1, sem_a2, sem_b2, sem_h,
):
    c = lax.axis_index("ctx")
    h = lax.axis_index("head")
    y, z, x = c // (NZ * NX), (c // NX) % NZ, c % NX
    xh, core = h // 2, h % 2
    yx = y * NX + x

    def dev(dy=0, dz=0, dx=0, dxh=0, dcore=0):
        ty, tz, tx = (y + dy) % NY, (z + dz) % NZ, (x + dx) % NX
        return ((ty * NZ + tz) * NX + tx, (xh + dxh) % 2 * 2 + (core + dcore) % 2)

    def send(src, dst, sems, i, device):
        copy = pltpu.make_async_remote_copy(
            src_ref=src, dst_ref=dst, send_sem=sems.at[0, i], recv_sem=sems.at[1, i],
            device_id=device, device_id_type=MESH,
        )
        copy.start()
        return copy

    def fetch(src, dst, i):
        copy = pltpu.make_async_copy(src, dst, sem_in.at[i])
        copy.start()
        return copy

    get_q = fetch(q_in, q_raw, 0)
    get_k = fetch(ck_in, k_all.at[0], 1)
    get_v = fetch(cv_in, v_all.at[0], 2)
    get_w = fetch(w_in, w_all, 3)

    barrier = pltpu.get_barrier_semaphore()
    peers = [dict(dz=d) for d in range(1, NZ)]
    peers += [dict(dy=dy, dx=dx) for dy, dx in YX[1:]]
    peers += [dict(dcore=1), dict(dxh=1)]
    for p in peers:
        pl.semaphore_signal(barrier, inc=1, device_id=dev(**p), device_id_type=MESH)

    turn[z, yx] = jnp.concatenate(
        [tk_ref[...].astype(F32), tv_ref[...].astype(F32)], axis=0
    ).astype(BF16)
    get_q.wait()
    i0, i1 = iota((128, 128), 0), iota((128, 128), 1)
    order = (i1 == (i0 % ROWS) * GROUP + i0 // ROWS).astype(BF16)
    mine = mm(order, q_raw[...]).astype(BF16).reshape(NZ, 16, HEAD)
    q_send[...] = mine
    q_all[:, z] = mine
    eye = (i0 == i1).astype(BF16)

    pl.semaphore_wait(barrier, len(peers))

    q_copies = [
        send(q_send, q_all.at[:, z], sem_q, d - 1, dev(dz=d)) for d in range(1, NZ)
    ]
    t_copies, kv_copies = [], {}
    for r, (dy, dx) in enumerate(YX):
        if r == 0:
            continue
        back = YX.index(((NY - dy) % NY, dx))
        t_copies.append(
            send(turn.at[z, yx], turn.at[z, yx], sem_t, r, dev(dy=dy, dx=dx))
        )
        kv_copies[r] = (
            send(ck_in, k_all.at[back], sem_kv, 2 * back, dev(dy=dy, dx=dx)),
            send(cv_in, v_all.at[back], sem_kv, 2 * back + 1, dev(dy=dy, dx=dx)),
        )

    def arrived(sems, i, ref):
        pltpu.make_async_copy(ref, ref, sems.at[1, i]).wait()

    tokens = NYX * ROWS
    t0, t1 = iota((tokens, 128), 0), iota((tokens, 128), 1)
    docs = doc_ref[...]
    doc_wide = jnp.concatenate(
        [jnp.broadcast_to(docs[i : i + 1], (16, 128)) for i in range(NY)], axis=0
    )
    key_doc = jnp.sum(
        jnp.where(t1 == 16 * z + t0 % 16, doc_wide, 0), axis=1, keepdims=True
    )
    key_pos = 128 * (t0 // 16) + 16 * z + t0 % 16
    doc_mine = jnp.sum(jnp.where(iota((NY, 128), 0) == y, docs, 0), axis=0, keepdims=True)
    seen = i0 == 16 * (i1 // 16) + 8 * x + i1 % 8
    query_doc = mm(
        jnp.broadcast_to(doc_mine, (16, 128)).astype(BF16), seen.astype(BF16)
    )[:1].astype(jnp.int32)
    query_pos = 128 * y + 16 * (t1 // 16) + 8 * x + t1 % 8
    see = (key_pos <= query_pos) & (key_doc == query_doc)
    see = jnp.where(see, 0.0, NEG)
    see = jnp.concatenate([see, see], axis=1)

    pick_k = (t1 == (t0 // ROWS) * 16 + t0 % ROWS).astype(BF16)
    pick_v = (t1 == (t0 // ROWS) * 16 + ROWS + t0 % ROWS).astype(BF16)

    for i, cp in enumerate(q_copies):
        cp.wait()

    for g, pair in enumerate(PAIRS):
        for j in range(2):
            r = 2 * g + j
            if r == 0:
                get_k.wait()
                get_v.wait()
            else:
                arrived(sem_kv, 2 * r, k_all.at[r])
                arrived(sem_kv, 2 * r + 1, v_all.at[r])
        vt_all[g, :HEAD] = nt(eye, v_all[2 * g : 2 * g + 2].reshape(2 * KEYS, HEAD)).astype(BF16)
        vt_all[g, HEAD:] = jnp.ones((16, 2 * KEYS), BF16)
        biases = []
        for dy, dx in pair:
            source = ((y + dy) % NY * NZ + z) * NX + (x + dx) % NX
            for b in range(2):
                biases.append(jnp.where(mask_ref[y, 2 * source + b] == 1, 0.0, NEG))
        last = g == len(PAIRS) - 1
        if last:
            for r in range(1, NYX):
                t_copies[r - 1].wait()
            fresh = turn[z].reshape(128, HEAD)
            turn_k = mm(pick_k, fresh).astype(BF16)
            turn_v = nt(eye, mm(pick_v, fresh).astype(BF16)).astype(BF16)
            turn_v = jnp.concatenate([turn_v, jnp.ones((16, tokens), BF16)], axis=0)
            tt_copies = [
                send(turn.at[z], turn.at[z], sem_tt, d - 1, dev(dz=d)) for d in range(1, NZ)
            ]

        def block(i, carry, g=g, biases=biases, last=last):
            q = q_all[pl.ds(2 * i, 2)].reshape(256, HEAD)
            s = nt(k_all[2 * g : 2 * g + 2].reshape(2 * KEYS, HEAD), q)
            parts = [s[128 * b : 128 * (b + 1)] for b in range(4)]
            tops = [
                jnp.max(p, axis=0, keepdims=True) * SCALE + bias for p, bias in zip(parts, biases)
            ]
            if last:
                ts = nt(turn_k, q) * SCALE + see
                tops.append(jnp.max(ts, axis=0, keepdims=True))
            top = tops[0]
            for t in tops[1:]:
                top = jnp.maximum(top, t)
            if g == 0:
                top = jnp.maximum(top, FLOOR)
            else:
                old = peak[i, :1]
                top = jnp.maximum(top, old)
            p = jnp.concatenate(
                [
                    jnp.exp2(p * SCALE - (top - bias)).astype(BF16)
                    for p, bias in zip(parts, biases)
                ],
                axis=0,
            )
            o = mm(vt_all[g], p)
            if last:
                o = o + mm(turn_v, jnp.exp2(ts - top).astype(BF16))
            if g > 0:
                o = o + acc[i] * jnp.exp2(old - top)
            if last:
                for j in range(2):
                    at = 2 * i + j
                    lanes = slice(128 * j, 128 * (j + 1))
                    o_send[at] = o[:HEAD, lanes].astype(BF16)
                    st_send[at] = jnp.concatenate(
                        [top[:, lanes], o[HEAD : HEAD + 7, lanes]], axis=0
                    )
            else:
                acc[i] = o
                peak[i] = jnp.broadcast_to(top, (8, 256))
            return carry

        lax.fori_loop(0, 4, block, 0)

    rs_copies = []
    for d in range(1, NZ):
        to = (z + d) % NZ
        rs_copies.append(send(st_send.at[to], st_recv.at[z], sem_rs, 2 * d - 2, dev(dz=d)))
        rs_copies.append(send(o_send.at[to], o_recv.at[z], sem_rs, 2 * d - 1, dev(dz=d)))
    o_recv[z] = o_send[z]
    st_recv[z] = st_send[z]
    for cp in rs_copies:
        cp.wait()
    stats = [st_recv[j] for j in range(NZ)]
    top = stats[0][:1]
    for st in stats[1:]:
        top = jnp.maximum(top, st[:1])
    den, num = 0.0, 0.0
    for j, st in enumerate(stats):
        factor = jnp.exp2(st[:1] - top)
        den = den + factor * st[1:2]
        num = num + factor * o_recv[j].astype(F32)
    att = (num * (1.0 / den)).T.reshape(NZ, 2, ROWS, HEAD)
    att = jnp.concatenate(
        [att[:, 0].reshape(64, HEAD), att[:, 1].reshape(64, HEAD)], axis=1
    ).astype(BF16)
    part_a[z, yx] = att[:32]
    part_b[z, yx] = att[32:]

    a1 = [
        send(part_a.at[z, yx], part_a.at[z, yx], sem_a1, r, dev(dy=dy, dx=dx))
        for r, (dy, dx) in enumerate(YX)
        if r
    ]
    b1 = [
        send(part_b.at[z, yx], part_b.at[z, yx], sem_b1, d, dev(dz=d)) for d in range(1, NZ)
    ]
    get_w.wait()

    def project(part, z_of, row):
        terms[row] += mm(
            part[z_of].reshape(256, 256), w_all[pl.ds(pl.multiple_of(z_of * 256, 256), 256)]
        )

    terms[...] = jnp.zeros_like(terms)
    for cp in a1:
        cp.wait()

    def hop(step, way):
        at = (z - step * way) % NZ
        if step < 3:
            ref = part_a.at[at]
        else:
            ref = part_a.at[at, pl.ds(0, 4) if way == 1 else pl.ds(4, 4)]
        return send(ref, ref, sem_a2, 2 * step + (way + 1) // 2, dev(dz=way))

    right, left = hop(0, 1), hop(0, -1)
    for cp in b1:
        cp.wait()
    b2 = [
        send(part_b.at[:, yx], part_b.at[:, yx], sem_b2, r, dev(dy=dy, dx=dx))
        for r, (dy, dx) in enumerate(YX)
        if r
    ]
    project(part_a, z, 0)
    for step in range(1, 4):
        right.wait()
        left.wait()
        right, left = hop(step, 1), hop(step, -1)
        project(part_a, (z - step) % NZ, 0)
        project(part_a, (z + step) % NZ, 0)

    for cp in tt_copies:
        cp.wait()
    col = iota((128, 1024), 1)
    piece = 32 * (col // 32 % 4) + 4 * (col // 128) + 2 * (col // 16 % 2) + col // 4 % 2
    spread = (iota((128, 1024), 0) == piece).astype(BF16)
    slot_of = mm(
        jnp.broadcast_to(slot_ref[...], (16, 128)).astype(BF16), spread
    ).astype(jnp.int32)
    row, col = iota((16, 1024), 0), iota((16, 1024), 1)
    chosen = (slot_of == 4 * c + row // 4) & (col % 4 == row % 4)
    every = turn[...].reshape(1024, HEAD)
    kind = col // 8 % 2
    ak_ref[...] = mm((chosen & (kind == 0)).astype(BF16), every).astype(BF16)
    av_ref[...] = mm((chosen & (kind == 1)).astype(BF16), every).astype(BF16)

    right.wait()
    left.wait()
    project(part_a, (z + 4) % NZ, 0)
    for cp in b2:
        cp.wait()
    for j in range(NZ):
        project(part_b, j, 1)

    blocks = [terms.at[:, pl.ds(pl.multiple_of((2 * a + 1 - core) * 64, 64), 64)] for a in range(2)]
    for a in range(2):
        h_send[a] = blocks[a][...].astype(BF16)
    to_core = send(h_send, h_recv, sem_h, 0, dev(dcore=1))
    to_core.wait()

    def kept(a):
        rows = terms.at[:, pl.ds(pl.multiple_of((2 * a + core) * 64, 64), 64)]
        return rows[...] + h_recv[a].astype(F32)

    h_send[0] = kept(1 - xh).astype(BF16)
    to_chip = send(h_send.at[0], x_recv, sem_h, 1, dev(dxh=1))
    own = kept(xh)
    to_chip.wait()
    total = own + x_recv[...].astype(F32)
    for half in range(2):
        for low in range(4):
            for tx in range(NX):
                out_ref[pl.ds(16 * (4 * half + low) + 8 * tx, 8)] = total[
                    half, 32 * tx + 8 * low : 32 * tx + 8 * low + 8
                ]
    for sent in kv_copies.values():
        for cp in sent:
            cp.wait_send()


def on_device(
    queries, cache_keys, stored_cache_values, turn_keys, turn_values,
    block_mask, doc_ids, slot_ids, out_weight,
):
    anywhere = pl.BlockSpec(memory_space=pl.ANY)
    vmem = pl.BlockSpec(memory_space=pltpu.VMEM)
    smem = pl.BlockSpec(memory_space=pltpu.SMEM)
    sems = lambda n: pltpu.SemaphoreType.DMA((2, n))
    layer_out, append_keys, append_values = pl.pallas_call(
        kernel,
        out_shape=(
            jax.ShapeDtypeStruct((128, 256), F32),
            jax.ShapeDtypeStruct((16, HEAD), BF16),
            jax.ShapeDtypeStruct((16, HEAD), BF16),
        ),
        in_specs=[anywhere] * 4 + [vmem] * 4 + [smem],
        out_specs=(vmem, vmem, vmem),
        scratch_shapes=[
            pltpu.VMEM((128, HEAD), BF16),
            pltpu.VMEM((NZ, 16, HEAD), BF16),
            pltpu.VMEM((NZ, NZ, 16, HEAD), BF16),
            pltpu.VMEM((NYX, KEYS, HEAD), BF16),
            pltpu.VMEM((NYX, KEYS, HEAD), BF16),
            pltpu.VMEM((4, HEAD + 16, 2 * KEYS), BF16),
            pltpu.VMEM((2048, 256), BF16),
            pltpu.VMEM((NZ, NYX, 16, HEAD), BF16),
            pltpu.VMEM((4, 8, 256), F32),
            pltpu.VMEM((4, HEAD + 16, 256), F32),
            pltpu.VMEM((NZ, HEAD, 128), BF16),
            pltpu.VMEM((NZ, 8, 128), F32),
            pltpu.VMEM((NZ, HEAD, 128), BF16),
            pltpu.VMEM((NZ, 8, 128), F32),
            pltpu.VMEM((NZ, NYX, 32, 256), BF16),
            pltpu.VMEM((NZ, NYX, 32, 256), BF16),
            pltpu.VMEM((2, 256, 256), F32),
            pltpu.VMEM((2, 2, 64, 256), BF16),
            pltpu.VMEM((2, 2, 64, 256), BF16),
            pltpu.VMEM((2, 64, 256), BF16),
            pltpu.SemaphoreType.DMA((4,)),
            sems(7), sems(16), sems(8), sems(7), sems(14), sems(8), sems(8), sems(8), sems(8), sems(2),
        ],
        compiler_params=pltpu.CompilerParams(
            collective_id=0, has_side_effects=True, vmem_limit_bytes=32 * 1024 * 1024
        ),
        name="turn_attention",
    )(
        queries.reshape(128, HEAD),
        cache_keys.reshape(KEYS, HEAD),
        stored_cache_values.reshape(KEYS, HEAD),
        out_weight,
        turn_keys.reshape(ROWS, HEAD),
        turn_values.reshape(ROWS, HEAD),
        doc_ids.reshape(NY, 128),
        slot_ids.reshape(1, 128),
        block_mask,
    )
    return (
        layer_out,
        append_keys.reshape(16, 1, HEAD),
        append_values.reshape(16, 1, HEAD),
    )


def solution(mesh):
    placed = (
        P("ctx", "head", None),
        P("ctx", "head", None),
        P("ctx", "head", None),
        P("ctx", "head", None),
        P("ctx", "head", None),
        P(),
        P(),
        P(),
        P("head", "ctx"),
    )
    return jax.shard_map(
        on_device,
        mesh=mesh,
        in_specs=placed,
        out_specs=(P("head", "ctx"), P("ctx", "head", None), P("ctx", "head", None)),
        check_vma=False,
    )
```

```python
import math

import jax
import jax.numpy as jnp
from jax import lax
from jax.experimental import pallas as pl
from jax.experimental.pallas import tpu as pltpu
from jax.sharding import PartitionSpec as P

MESH = pl.DeviceIdType.MESH
F32 = jnp.float32
BF16 = jnp.bfloat16

NY, NZ, NX = 4, 8, 2
NYX = NY * NX
NH = 4
HEAD = 128
KEYS = 256
GROUP = 16
ROWS = 8
NEG = -1e30
FLOOR = -1e29
SCALE = math.log2(math.e) / math.sqrt(HEAD)

YX = [(0, 0), (0, 1), (1, 0), (1, 1), (3, 0), (3, 1), (2, 0), (2, 1)]
YX_ORDER = [1, 2, 4, 3, 5, 6, 7]
ZS = [0, 1, 7, 2, 6, 3, 5, 4]
Z_ORDER = [1, 7, 2, 6, 3, 5, 4]
Z_BATCHES = [(0, 1), (1, 3), (3, 5), (5, 8)]


def nt(a, b):
    return lax.dot_general(a, b, (((1,), (1,)), ((), ())), preferred_element_type=F32)


def mm(a, b):
    return jnp.dot(a, b, preferred_element_type=F32)


def iota(shape, dim):
    return lax.broadcasted_iota(jnp.int32, shape, dim)


def back_yx(r):
    dy, dx = YX[r]
    return YX.index(((NY - dy) % NY, dx))


def kernel(
    q_in, ck_in, cv_in, w_in, tk_in, tv_in, doc_in, slot_in, mask_in,
    out_ref, ak_ref, av_ref,
    q_raw, q_send, q_all, k_all, v_all, v_wide, w_all, turn, tk, tv, docs_ref, slots_ref, mask_ref,
    peak, acc, o_send, st_send, o_recv, st_recv, part_a, part_b, sum_a, sum_b,
    ha_send, ha_recv, hb_send, hb_recv,
    sem_in, sem_q, sem_kv, sem_t, sem_tt, sem_rs, sem_a1, sem_b1, sem_a2, sem_b2, sem_h,
):
    c = lax.axis_index("ctx")
    h = lax.axis_index("head")
    y, z, x = c // (NZ * NX), (c // NX) % NZ, c % NX
    yx = y * NX + x

    def dev(dy=0, dz=0, dx=0, dh=0):
        ty, tz, tx = (y + dy) % NY, (z + dz) % NZ, (x + dx) % NX
        return ((ty * NZ + tz) * NX + tx, (h + dh) % NH)

    def to_yx(r):
        return dev(dy=YX[r][0], dx=YX[r][1])

    def send(src, dst, sems, i, device):
        copy = pltpu.make_async_remote_copy(
            src_ref=src, dst_ref=dst, send_sem=sems.at[0, i], recv_sem=sems.at[1, i],
            device_id=device, device_id_type=MESH,
        )
        copy.start()
        return copy

    def arrived(ref, sems, i):
        pltpu.make_async_copy(ref, ref, sems.at[1, i]).wait()

    def fetch(src, dst, i):
        copy = pltpu.make_async_copy(src, dst, sem_in.at[i])
        copy.start()
        return copy

    get_q = fetch(q_in, q_raw, 0)
    get_small = [
        fetch(tk_in, tk, 1), fetch(tv_in, tv, 2), fetch(doc_in, docs_ref, 3),
        fetch(slot_in, slots_ref, 4), fetch(mask_in, mask_ref, 5),
    ]
    get_kv = [fetch(ck_in, k_all.at[0], 6), fetch(cv_in, v_all.at[0], 7)]
    get_w = fetch(w_in, w_all, 8)

    barrier = pltpu.get_barrier_semaphore()
    peers = [to_yx(r) for r in YX_ORDER] + [dev(dz=d) for d in Z_ORDER]
    peers += [dev(dh=d) for d in range(1, NH)]
    for p in peers:
        pl.semaphore_signal(barrier, inc=1, device_id=p, device_id_type=MESH)

    get_q.wait()
    i0, i1 = iota((128, 128), 0), iota((128, 128), 1)
    order = (i1 == (i0 % ROWS) * GROUP + i0 // ROWS).astype(BF16)
    mine = mm(order, q_raw[...]).astype(BF16).reshape(NZ, 16, HEAD)
    q_send[...] = mine
    q_all[:, z] = mine
    for cp in get_small:
        cp.wait()
    turn[z, yx] = jnp.concatenate([tk[...].astype(F32), tv[...].astype(F32)], axis=0).astype(BF16)

    pl.semaphore_wait(barrier, len(peers))

    q_copies = [send(q_send, q_all.at[:, z], sem_q, d, dev(dz=d)) for d in Z_ORDER]
    kv_copies, t_copies = [], []
    for r in YX_ORDER:
        b = back_yx(r)
        kv_copies.append(send(ck_in, k_all.at[b], sem_kv, 2 * b, to_yx(r)))
        kv_copies.append(send(cv_in, v_all.at[b], sem_kv, 2 * b + 1, to_yx(r)))
        t_copies.append(send(turn.at[z, yx], turn.at[z, yx], sem_t, r, to_yx(r)))

    docs = docs_ref[...]
    key_token = 16 * z + 8 * (i1 // 16 % 2) + i1 % 8
    by_y = mm(
        jnp.concatenate([docs.astype(F32), jnp.zeros((12, 128), F32)], axis=0).astype(BF16),
        (i0 == key_token).astype(BF16),
    )
    key_doc = jnp.sum(
        jnp.where(iota((16, 128), 0) == iota((16, 128), 1) // 32, by_y, 0.0), axis=0, keepdims=True
    )
    doc_mine = jnp.sum(
        jnp.where(iota((NY, 128), 0) == y, docs, 0), axis=0, keepdims=True
    ).astype(F32)
    query_token = 16 * (i0 // 16) + 8 * x + i0 % 8
    query_doc = jnp.sum(jnp.where(i1 == query_token, doc_mine, 0.0), axis=1, keepdims=True)
    see = (
        (128 * (i1 // 32) + key_token <= 128 * y + query_token)
        & (key_doc == query_doc)
        & (i1 // 8 % 2 == 0)
    )
    see = jnp.where(see, 0.0, NEG)
    see = jnp.concatenate([see, see], axis=0)
    diagonal = i0 == i1

    for cp in q_copies:
        cp.wait()

    for g in range(4):
        for r in (2 * g, 2 * g + 1):
            if r == 0:
                for cp in get_kv:
                    cp.wait()
            else:
                arrived(k_all.at[r], sem_kv, 2 * r)
                arrived(v_all.at[r], sem_kv, 2 * r + 1)
        v_wide[:, :HEAD] = v_all[2 * g : 2 * g + 2].reshape(2 * KEYS, HEAD)
        v_wide[:, HEAD:] = jnp.ones((2 * KEYS, HEAD), BF16)
        biases = []
        for dy, dx in YX[2 * g : 2 * g + 2]:
            source = ((y + dy) % NY * NZ + z) * NX + (x + dx) % NX
            for b in range(2):
                biases.append(jnp.where(mask_ref[y, 2 * source + b] == 1, 0.0, NEG))
        last = g == 3
        if last:
            for cp in t_copies:
                cp.wait()
            fresh = turn[z].reshape(128, HEAD)
            fresh_v = mm((i1 == i0 + 8).astype(BF16), fresh).astype(BF16)
            fresh_v = jnp.concatenate([fresh_v, jnp.ones((128, HEAD), BF16)], axis=1)
            tt_copies = [send(turn.at[z], turn.at[z], sem_tt, d, dev(dz=d)) for d in Z_ORDER]
        for i in range(4):
            q = q_all[2 * i : 2 * i + 2].reshape(256, HEAD)
            s = nt(q, k_all[2 * g : 2 * g + 2].reshape(2 * KEYS, HEAD))
            parts = [s[:, 128 * b : 128 * (b + 1)] * SCALE + biases[b] for b in range(4)]
            values = v_wide[...]
            if last:
                parts.append(nt(q, fresh) * SCALE + see)
                values = jnp.concatenate([values, fresh_v], axis=0)
            top = parts[0]
            for p in parts[1:]:
                top = jnp.maximum(top, p)
            top = jnp.broadcast_to(jnp.max(top, axis=1, keepdims=True), (256, 128))
            old = FLOOR if g == 0 else peak[i]
            top = jnp.maximum(top, old)
            p = jnp.concatenate([jnp.exp2(p - top).astype(BF16) for p in parts], axis=1)
            o = mm(p, values)
            if g > 0:
                keep = jnp.exp2(old - top)
                o = o + acc[i] * jnp.concatenate([keep, keep], axis=1)
            if not last:
                acc[i] = o
                peak[i] = top
                continue
            for j in range(2):
                rows = slice(128 * j, 128 * (j + 1))
                o_send[2 * i + j] = o[rows, :HEAD].astype(BF16)
                st_send[2 * i + j] = jnp.concatenate(
                    [
                        jnp.sum(jnp.where(diagonal, top[rows], 0.0), axis=0, keepdims=True),
                        jnp.sum(jnp.where(diagonal, o[rows, HEAD:], 0.0), axis=0, keepdims=True),
                        jnp.zeros((6, 128), F32),
                    ],
                    axis=0,
                )

    halves = (pl.ds(0, 64), pl.ds(64, 64))
    rs = [[], []]
    for d in Z_ORDER:
        to = (z + d) % NZ
        rs[0].append(send(st_send.at[to], st_recv.at[z], sem_rs, d, dev(dz=d)))
    for half in range(2):
        for d in Z_ORDER:
            to = (z + d) % NZ
            rs[half].append(
                send(
                    o_send.at[to, halves[half]], o_recv.at[z, halves[half]],
                    sem_rs, 8 * (half + 1) + d, dev(dz=d),
                )
            )
    o_recv[z] = o_send[z]
    st_recv[z] = st_send[z]
    for cp in rs[0]:
        cp.wait()
    peaks = jnp.concatenate([st_recv[j, 0:1] for j in range(NZ)], axis=0)
    totals = jnp.concatenate([st_recv[j, 1:2] for j in range(NZ)], axis=0)
    factor = jnp.exp2(peaks - jnp.max(peaks, axis=0, keepdims=True))
    factor = factor / jnp.sum(factor * totals, axis=0, keepdims=True)
    factor = jnp.concatenate([factor, jnp.zeros((120, 128), F32)], axis=0).T

    def attended(half):
        rows = slice(64 * half, 64 * (half + 1))
        num = 0.0
        for j in range(NZ):
            num = num + factor[rows, j : j + 1] * o_recv[j, halves[half]].astype(F32)
        num = num.reshape(4, 2, ROWS, HEAD)
        return jnp.concatenate(
            [num[:, 0].reshape(32, HEAD), num[:, 1].reshape(32, HEAD)], axis=1
        ).astype(BF16)

    part_a[0, 0] = attended(0)
    a1 = {r: send(part_a.at[0, 0], part_a.at[0, back_yx(r)], sem_a1, back_yx(r), to_yx(r)) for r in YX_ORDER}
    for cp in rs[1]:
        cp.wait()
    part_b[0, 0] = attended(1)
    b1 = [
        send(part_b.at[0, 0], part_b.at[ZS.index(NZ - d), 0], sem_b1, ZS.index(NZ - d), dev(dz=d))
        for d in Z_ORDER
    ]
    b2, a2 = [], []

    def spread(batch):
        lo, hi = Z_BATCHES[batch]
        for s in range(lo, hi):
            if s:
                arrived(part_b.at[s, 0], sem_b1, s)
        for r in YX_ORDER:
            b = back_yx(r)
            b2.append(
                send(
                    part_b.at[pl.ds(lo, hi - lo), 0], part_b.at[pl.ds(lo, hi - lo), b],
                    sem_b2, 8 * batch + b, to_yx(r),
                )
            )

    def spread_arrived(batch):
        lo, hi = Z_BATCHES[batch]
        for r in YX_ORDER:
            arrived(part_b.at[pl.ds(lo, hi - lo), r], sem_b2, 8 * batch + r)

    def piece(slot, p):
        return part_a.at[slot, pl.ds(2 * p, 2)]

    def index(hop, way, p):
        return 8 * hop + 4 * way + p

    def pass_on(hop, p, both=True):
        for way, (step, src, dst) in enumerate((
            (1, (NZ - hop) % NZ, NZ - 1 - hop), (-1, hop, hop + 1),
        )):
            if hop == 3:
                if p // 2 != way:
                    continue
                step, src, dst = 2 * step, (6, 2)[way], 4
            a2.append(send(piece(src, p), piece(dst, p), sem_a2, index(hop, way, p), dev(dz=step)))

    def passed(hop, p):
        for way in range(2):
            dst = (NZ - 1 - hop, hop + 1)[way]
            if hop == 3:
                if p // 2 != way:
                    continue
                dst = 4
            arrived(piece(dst, p), sem_a2, index(hop, way, p))

    def weight(dz):
        at = pl.multiple_of((z + dz) % NZ * 256, 256)
        return w_all[pl.ds(at, 256)]

    def project_a(slot):
        part = mm(part_a[slot].reshape(256, 256), weight(slot))
        sum_a[...] = part if slot == 0 else sum_a[...] + part

    def project_b(batch):
        lo, hi = Z_BATCHES[batch]
        part = 0.0
        for s in range(lo, hi):
            part = part + mm(part_b[s].reshape(256, 256), weight(ZS[s]))
        sum_b[...] = part if batch == 0 else sum_b[...] + part

    spread(0)
    for p in range(4):
        for r in (2 * p, 2 * p + 1):
            if r:
                arrived(part_a.at[0, r], sem_a1, r)
        pass_on(0, p)
        if p == 1:
            spread(1)
    spread(2)
    get_w.wait()
    project_a(0)
    for p in range(4):
        passed(0, p)
        pass_on(1, p)
        if p == 0:
            spread(3)
    spread_arrived(0)
    project_a(1)
    project_a(7)
    project_b(0)
    for p in range(4):
        passed(1, p)
        pass_on(2, p)
        pass_on(3, p)
    project_a(2)
    project_a(6)

    for cp in tt_copies:
        cp.wait()
    col = iota((128, 1024), 1)
    of_piece = 32 * (col // 32 % 4) + 4 * (col // 128) + 2 * (col // 16 % 2) + col // 4 % 2
    slot_of = mm(
        jnp.broadcast_to(slots_ref[...], (16, 128)).astype(BF16),
        (iota((128, 1024), 0) == of_piece).astype(BF16),
    ).astype(jnp.int32)
    row, col = iota((16, 1024), 0), iota((16, 1024), 1)
    chosen = (slot_of == 4 * c + row // 4) & (col % 4 == row % 4)
    every = turn[...].reshape(1024, HEAD)
    kind = col // 8 % 2
    ak_ref[...] = mm((chosen & (kind == 0)).astype(BF16), every).astype(BF16)
    av_ref[...] = mm((chosen & (kind == 1)).astype(BF16), every).astype(BF16)

    def rows_of(head):
        dy = (head + NY - y) % NY
        return pl.ds(pl.multiple_of(64 * jnp.where(dy >= 2, 5 - dy, dy), 64), 64)

    def share(total, sent, got, base):
        copies = []
        for d in (2, 3, 1):
            sent[d - 1] = total[rows_of((h + d) % NH)].astype(BF16)
            copies.append(send(sent.at[d - 1], got.at[3 - d], sem_h, base + 3 - d, dev(dh=d)))
        return copies

    def finish(total, got, copies, first):
        for cp in copies:
            cp.wait()
        whole = total[rows_of(h)]
        for j in range(3):
            whole = whole + got[j].astype(F32)
        for dx in range(NX):
            for j in range(4):
                at = 16 * (first + j) + 8 * ((x + dx) % NX)
                out_ref[pl.ds(pl.multiple_of(at, 8), 8)] = whole[
                    32 * dx + 8 * j : 32 * dx + 8 * j + 8
                ]

    for batch in range(1, 4):
        spread_arrived(batch)
        project_b(batch)
    to_b = share(sum_b, hb_send, hb_recv, 0)
    for p in range(4):
        passed(2, p)
    project_a(3)
    project_a(5)
    for p in range(4):
        passed(3, p)
    project_a(4)
    to_a = share(sum_a, ha_send, ha_recv, 3)
    finish(sum_b, hb_recv, to_b, 4)
    for cp in kv_copies + list(a1.values()) + b1 + b2 + a2:
        cp.wait_send()
    finish(sum_a, ha_recv, to_a, 0)


def on_device(
    queries, cache_keys, stored_cache_values, turn_keys, turn_values,
    block_mask, doc_ids, slot_ids, out_weight,
):
    anywhere = pl.BlockSpec(memory_space=pl.ANY)
    vmem = pl.BlockSpec(memory_space=pltpu.VMEM)
    sems = lambda n: pltpu.SemaphoreType.DMA((2, n))
    layer_out, append_keys, append_values = pl.pallas_call(
        kernel,
        out_shape=(
            jax.ShapeDtypeStruct((128, 256), F32),
            jax.ShapeDtypeStruct((16, HEAD), BF16),
            jax.ShapeDtypeStruct((16, HEAD), BF16),
        ),
        in_specs=[anywhere] * 9,
        out_specs=(vmem, vmem, vmem),
        scratch_shapes=[
            pltpu.VMEM((128, HEAD), BF16),
            pltpu.VMEM((NZ, 16, HEAD), BF16),
            pltpu.VMEM((NZ, NZ, 16, HEAD), BF16),
            pltpu.VMEM((NYX, KEYS, HEAD), BF16),
            pltpu.VMEM((NYX, KEYS, HEAD), BF16),
            pltpu.VMEM((2 * KEYS, 2 * HEAD), BF16),
            pltpu.VMEM((2048, 256), BF16),
            pltpu.VMEM((NZ, NYX, 16, HEAD), BF16),
            pltpu.VMEM((ROWS, HEAD), BF16),
            pltpu.VMEM((ROWS, HEAD), BF16),
            pltpu.VMEM((NY, 128), jnp.int32),
            pltpu.VMEM((1, 128), jnp.int32),
            pltpu.SMEM((NY, 128), jnp.int32),
            pltpu.VMEM((4, 256, 128), F32),
            pltpu.VMEM((4, 256, 256), F32),
            pltpu.VMEM((NZ, 128, HEAD), BF16),
            pltpu.VMEM((NZ, 8, 128), F32),
            pltpu.VMEM((NZ, 128, HEAD), BF16),
            pltpu.VMEM((NZ, 8, 128), F32),
            pltpu.VMEM((NZ, NYX, 32, 256), BF16),
            pltpu.VMEM((NZ, NYX, 32, 256), BF16),
            pltpu.VMEM((256, 256), F32),
            pltpu.VMEM((256, 256), F32),
            pltpu.VMEM((3, 64, 256), BF16),
            pltpu.VMEM((3, 64, 256), BF16),
            pltpu.VMEM((3, 64, 256), BF16),
            pltpu.VMEM((3, 64, 256), BF16),
            pltpu.SemaphoreType.DMA((9,)),
            sems(8), sems(16), sems(8), sems(8), sems(24), sems(8), sems(8), sems(32), sems(32), sems(6),
        ],
        compiler_params=pltpu.CompilerParams(
            collective_id=0, has_side_effects=True, vmem_limit_bytes=60 * 1024 * 1024
        ),
        name="turn_attention",
    )(
        queries.reshape(128, HEAD),
        cache_keys.reshape(KEYS, HEAD),
        stored_cache_values.reshape(KEYS, HEAD),
        out_weight,
        turn_keys.reshape(ROWS, HEAD),
        turn_values.reshape(ROWS, HEAD),
        doc_ids.reshape(NY, 128),
        slot_ids.reshape(1, 128),
        block_mask,
    )
    return (
        layer_out,
        append_keys.reshape(16, 1, HEAD),
        append_values.reshape(16, 1, HEAD),
    )


def solution(mesh):
    placed = (
        P("ctx", "head", None),
        P("ctx", "head", None),
        P("ctx", "head", None),
        P("ctx", "head", None),
        P("ctx", "head", None),
        P(),
        P(),
        P(),
        P("head", "ctx"),
    )
    return jax.shard_map(
        on_device,
        mesh=mesh,
        in_specs=placed,
        out_specs=(P("head", "ctx"), P("ctx", "head", None), P("ctx", "head", None)),
        check_vma=False,
    )
```

```python
import math

import jax
import jax.numpy as jnp
from jax import lax
from jax.experimental import pallas as pl
from jax.experimental.pallas import tpu as pltpu
from jax.sharding import PartitionSpec as P

MESH = pl.DeviceIdType.MESH
F32 = jnp.float32
BF16 = jnp.bfloat16

NY, NZ, NX = 4, 8, 2
NYX = NY * NX
NH = 4
HEAD = 128
KEYS = 256
GROUP = 16
ROWS = 8
NEG = -1e30
FLOOR = -1e29
SCALE = math.log2(math.e) / math.sqrt(HEAD)

YX = [(0, 0), (0, 1), (1, 0), (1, 1), (3, 0), (3, 1), (2, 0), (2, 1)]
YX_ORDER = [1, 2, 4, 3, 5, 6, 7]
ZS = [0, 1, 7, 2, 6, 3, 5, 4]
Z_ORDER = [1, 7, 2, 6, 3, 5, 4]
Z_BATCHES = [(0, 1), (1, 3), (3, 5), (5, 8)]
KEY_GROUPS = [(0, 1), (2, 4), (6, 3), (5, 7)]
BLOCKS = [
    (0, 0), (0, 1), (1, 0), (1, 1), (0, 2), (1, 2), (2, 0), (2, 1), (2, 2), (0, 3), (1, 3), (2, 3),
    (3, 0), (3, 1), (3, 2), (3, 3),
]


def nt(a, b):
    return lax.dot_general(a, b, (((1,), (1,)), ((), ())), preferred_element_type=F32)


def mm(a, b):
    return jnp.dot(a, b, preferred_element_type=F32)


def iota(shape, dim):
    return lax.broadcasted_iota(jnp.int32, shape, dim)


def back_yx(r):
    dy, dx = YX[r]
    return YX.index(((NY - dy) % NY, dx))


def kernel(
    q_in, ck_in, cv_in, w_in, tk_in, tv_in, doc_in, slot_in, mask_in,
    out_ref, ak_ref, av_ref,
    q_raw, q_all, k_all, v_all, v_wide, w_all, turn_yx, turn_all, tk, tv, docs_ref, slots_ref, mask_ref,
    peak, acc, o_send, st_send, o_recv, st_recv, factors, part_a, part_b, sum_a, sum_b,
    ha_send, ha_recv, hb_send, hb_recv,
    sem_in, sem_q, sem_kv, sem_t, sem_tz, sem_tt, sem_rs, sem_a1, sem_b1, sem_a2, sem_b2, sem_h,
):
    c = lax.axis_index("ctx")
    h = lax.axis_index("head")
    y, z, x = c // (NZ * NX), (c // NX) % NZ, c % NX
    yx = y * NX + x

    def dev(dy=0, dz=0, dx=0, dh=0):
        ty, tz, tx = (y + dy) % NY, (z + dz) % NZ, (x + dx) % NX
        return ((ty * NZ + tz) * NX + tx, (h + dh) % NH)

    def to_yx(r):
        return dev(dy=YX[r][0], dx=YX[r][1])

    def send(src, dst, sems, i, device):
        copy = pltpu.make_async_remote_copy(
            src_ref=src, dst_ref=dst, send_sem=sems.at[0, i], recv_sem=sems.at[1, i],
            device_id=device, device_id_type=MESH,
        )
        copy.start()
        return copy

    def arrived(ref, sems, i):
        pltpu.make_async_copy(ref, ref, sems.at[1, i]).wait()

    def fetch(src, dst, i):
        copy = pltpu.make_async_copy(src, dst, sem_in.at[i])
        copy.start()
        return copy

    get_q = fetch(q_in, q_raw, 0)
    get_small = [
        fetch(tk_in, tk, 1), fetch(tv_in, tv, 2), fetch(doc_in, docs_ref, 3),
        fetch(slot_in, slots_ref, 4), fetch(mask_in, mask_ref, 5),
    ]
    get_kv = [fetch(ck_in, k_all.at[0], 6), fetch(cv_in, v_all.at[0], 7)]
    get_w = fetch(w_in, w_all, 8)

    barrier = pltpu.get_barrier_semaphore()
    peers = [to_yx(r) for r in YX_ORDER] + [dev(dz=d) for d in Z_ORDER]
    peers += [dev(dh=d) for d in range(1, NH)]
    for p in peers:
        pl.semaphore_signal(barrier, inc=1, device_id=p, device_id_type=MESH)

    get_q.wait()
    i0, i1 = iota((128, 128), 0), iota((128, 128), 1)
    order = (i1 == (i0 % ROWS) * GROUP + i0 // ROWS).astype(BF16)
    q_all[0] = mm(order, q_raw[...]).astype(BF16)
    for cp in get_small:
        cp.wait()
    mine = jnp.concatenate([tk[...].astype(F32), tv[...].astype(F32)], axis=0).astype(BF16)
    turn_yx[yx] = mine
    turn_all[z, yx] = mine

    pl.semaphore_wait(barrier, len(peers))

    def give_k(src, slot, device):
        return send(src, k_all.at[slot], sem_kv, 2 * slot, device)

    def give_v(src, slot, device):
        return send(src, v_all.at[slot], sem_kv, 2 * slot + 1, device)

    q_copies = {d: send(q_all.at[0], q_all.at[ZS.index(NZ - d)], sem_q, ZS.index(NZ - d), dev(dz=d)) for d in Z_ORDER}
    kv_copies = [give_v(cv_in, 1, to_yx(1))]
    for r in (2, 4, 6):
        kv_copies.append(give_k(ck_in, back_yx(r), to_yx(r)))
    kv_copies.append(give_k(ck_in, 1, to_yx(1)))
    for r in (2, 4, 6):
        kv_copies.append(give_v(cv_in, back_yx(r), to_yx(r)))
    t_copies = [send(turn_yx.at[yx], turn_yx.at[yx], sem_t, r, to_yx(r)) for r in YX_ORDER]
    tz_copies = [send(turn_yx.at[yx], turn_all.at[z, yx], sem_tz, d, dev(dz=d)) for d in Z_ORDER]

    docs = docs_ref[...]
    key_token = 16 * z + 8 * (i1 // 16 % 2) + i1 % 8
    by_y = mm(
        jnp.concatenate([docs.astype(F32), jnp.zeros((12, 128), F32)], axis=0).astype(BF16),
        (i0 == key_token).astype(BF16),
    )
    key_doc = jnp.sum(
        jnp.where(iota((16, 128), 0) == iota((16, 128), 1) // 32, by_y, 0.0), axis=0, keepdims=True
    )
    doc_mine = jnp.sum(
        jnp.where(iota((NY, 128), 0) == y, docs, 0), axis=0, keepdims=True
    ).astype(F32)
    right_key = (i1 // 8 % 2 == 0)

    def sight(slot):
        query_token = 16 * ((z + ZS[slot]) % NZ) + 8 * x + i0 % 8
        query_doc = jnp.sum(jnp.where(i1 == query_token, doc_mine, 0.0), axis=1, keepdims=True)
        see = (
            (128 * (i1 // 32) + key_token <= 128 * y + query_token)
            & (key_doc == query_doc)
            & right_key
        )
        return jnp.where(see, 0.0, NEG)

    diagonal = i0 == i1

    arrived(v_all.at[1], sem_kv, 3)
    for r in (2, 4, 6):
        kv_copies.append(give_v(v_all.at[1], back_yx(r + 1), to_yx(r)))
    for r in (2, 4, 6):
        arrived(k_all.at[r], sem_kv, 2 * r)
        kv_copies.append(give_k(k_all.at[r], r + 1, to_yx(1)))

    have = {("k", 2), ("k", 4), ("k", 6), ("v", 1)}
    biases = {}
    for g, i in BLOCKS:
        last = g == 3
        if i == 0:
            for j, r in enumerate(KEY_GROUPS[g]):
                if r == 0:
                    for cp in get_kv:
                        cp.wait()
                else:
                    if ("k", r) not in have:
                        arrived(k_all.at[r], sem_kv, 2 * r)
                    if ("v", r) not in have:
                        arrived(v_all.at[r], sem_kv, 2 * r + 1)
                v_wide[g, KEYS * j : KEYS * (j + 1), :HEAD] = v_all[r]
            v_wide[g, :, HEAD:] = jnp.ones((2 * KEYS, HEAD), BF16)
            biases[g] = []
            for r in KEY_GROUPS[g]:
                source = ((y + YX[r][0]) % NY * NZ + z) * NX + (x + YX[r][1]) % NX
                for b in range(2):
                    biases[g].append(jnp.where(mask_ref[y, 2 * source + b] == 1, 0.0, NEG))
            if last:
                for cp in t_copies:
                    cp.wait()
                fresh = turn_yx[...].reshape(128, HEAD)
                fresh_v = mm((i1 == i0 + 8).astype(BF16), fresh).astype(BF16)
                fresh_v = jnp.concatenate([fresh_v, jnp.ones((128, HEAD), BF16)], axis=1)
        if g == 0:
            for slot in (2 * i, 2 * i + 1):
                if slot:
                    arrived(q_all.at[slot], sem_q, slot)
        q = q_all[2 * i : 2 * i + 2].reshape(256, HEAD)
        parts = []
        for j, r in enumerate(KEY_GROUPS[g]):
            s = nt(q, k_all[r])
            parts += [
                s[:, :128] * SCALE + biases[g][2 * j], s[:, 128:] * SCALE + biases[g][2 * j + 1]
            ]
        values = v_wide[g]
        if last:
            see = jnp.concatenate([sight(2 * i), sight(2 * i + 1)], axis=0)
            parts.append(nt(q, fresh) * SCALE + see)
            values = jnp.concatenate([values, fresh_v], axis=0)
        top = parts[0]
        for p in parts[1:]:
            top = jnp.maximum(top, p)
        top = jnp.broadcast_to(jnp.max(top, axis=1, keepdims=True), (256, 128))
        old = FLOOR if g == 0 else peak[i]
        top = jnp.maximum(top, old)
        p = jnp.concatenate([jnp.exp2(p - top).astype(BF16) for p in parts], axis=1)
        o = mm(p, values)
        if g > 0:
            keep = jnp.exp2(old - top)
            o = o + acc[i] * jnp.concatenate([keep, keep], axis=1)
        if not last:
            acc[i] = o
            peak[i] = top
            continue
        for j in range(2):
            rows = slice(128 * j, 128 * (j + 1))
            of = (z + ZS[2 * i + j]) % NZ
            o_send[:, of] = o[rows, :HEAD].astype(BF16).reshape(NZ, 16, HEAD)
            st_send[pl.ds(of, 1)] = jnp.sum(
                jnp.where(diagonal, top[rows], 0.0), axis=0, keepdims=True
            )
            st_send[pl.ds(NZ + of, 1)] = jnp.sum(
                jnp.where(diagonal, o[rows, HEAD:], 0.0), axis=0, keepdims=True
            )

    halves = (pl.ds(0, 4), pl.ds(4, 4))
    rs = [[], []]
    for d in Z_ORDER:
        rs[0].append(send(st_send, st_recv.at[z], sem_rs, d, dev(dz=d)))
    for half in range(2):
        for d in Z_ORDER:
            rs[half].append(
                send(
                    o_send.at[(z + d) % NZ, halves[half]], o_recv.at[z, halves[half]],
                    sem_rs, 8 * (half + 1) + d, dev(dz=d),
                )
            )
    o_recv[z] = o_send[z]
    st_recv[z] = st_send[...]
    for cp in tz_copies:
        cp.wait()
    tt_copies = [send(turn_all.at[:, yx], turn_all.at[:, yx], sem_tt, r, to_yx(r)) for r in YX_ORDER]
    for cp in rs[0]:
        cp.wait()
    peaks, totals = st_recv[:, :NZ], st_recv[:, NZ:]
    factor = jnp.exp2(peaks - jnp.max(peaks, axis=0, keepdims=True))
    factor = factor / jnp.sum(factor * totals, axis=0, keepdims=True)
    factors[...] = jnp.concatenate(
        [factor.reshape(NZ * NZ, 128), jnp.zeros((128 - NZ * NZ, 128), F32)], axis=0
    ).T
    factor = factors[pl.ds(pl.multiple_of(16 * z, 16), 16)]

    def attended(half):
        out = []
        for of in range(4 * half, 4 * half + 4):
            num = 0.0
            for j in range(NZ):
                at = NZ * j + of
                num = num + factor[:, at : at + 1] * o_recv[j, of].astype(F32)
            out.append(jnp.concatenate([num[:ROWS], num[ROWS:]], axis=1))
        return jnp.concatenate(out, axis=0).astype(BF16)

    part_a[0, 0] = attended(0)
    a1 = {r: send(part_a.at[0, 0], part_a.at[0, back_yx(r)], sem_a1, back_yx(r), to_yx(r)) for r in YX_ORDER}
    for cp in rs[1]:
        cp.wait()
    part_b[0, 0] = attended(1)
    b1 = [
        send(part_b.at[0, 0], part_b.at[ZS.index(NZ - d), 0], sem_b1, ZS.index(NZ - d), dev(dz=d))
        for d in Z_ORDER
    ]
    b2, a2 = [], []

    def spread(batch):
        lo, hi = Z_BATCHES[batch]
        for s in range(lo, hi):
            if s:
                arrived(part_b.at[s, 0], sem_b1, s)
        for r in YX_ORDER:
            b = back_yx(r)
            b2.append(
                send(
                    part_b.at[pl.ds(lo, hi - lo), 0], part_b.at[pl.ds(lo, hi - lo), b],
                    sem_b2, 8 * batch + b, to_yx(r),
                )
            )

    def spread_arrived(batch):
        lo, hi = Z_BATCHES[batch]
        for r in YX_ORDER:
            arrived(part_b.at[pl.ds(lo, hi - lo), r], sem_b2, 8 * batch + r)

    def piece(slot, p):
        return part_a.at[slot, pl.ds(2 * p, 2)]

    def index(hop, way, p):
        return 8 * hop + 4 * way + p

    def pass_on(hop, p, both=True):
        for way, (step, src, dst) in enumerate((
            (1, (NZ - hop) % NZ, NZ - 1 - hop), (-1, hop, hop + 1),
        )):
            if hop == 3:
                if p // 2 != way:
                    continue
                step, src, dst = 2 * step, (6, 2)[way], 4
            a2.append(send(piece(src, p), piece(dst, p), sem_a2, index(hop, way, p), dev(dz=step)))

    def passed(hop, p):
        for way in range(2):
            dst = (NZ - 1 - hop, hop + 1)[way]
            if hop == 3:
                if p // 2 != way:
                    continue
                dst = 4
            arrived(piece(dst, p), sem_a2, index(hop, way, p))

    def weight(dz):
        at = pl.multiple_of((z + dz) % NZ * 256, 256)
        return w_all[pl.ds(at, 256)]

    def project_a(slot):
        part = mm(part_a[slot].reshape(256, 256), weight(slot))
        sum_a[...] = part if slot == 0 else sum_a[...] + part

    def project_b(batch):
        lo, hi = Z_BATCHES[batch]
        part = 0.0
        for s in range(lo, hi):
            part = part + mm(part_b[s].reshape(256, 256), weight(ZS[s]))
        sum_b[...] = part if batch == 0 else sum_b[...] + part

    spread(0)
    for p in range(4):
        for r in (2 * p, 2 * p + 1):
            if r:
                arrived(part_a.at[0, r], sem_a1, r)
        pass_on(0, p)
        if p == 1:
            spread(1)
    spread(2)
    get_w.wait()
    project_a(0)
    for p in range(4):
        passed(0, p)
        pass_on(1, p)
        if p == 0:
            spread(3)
    spread_arrived(0)
    project_a(1)
    project_a(7)
    project_b(0)
    for p in range(4):
        passed(1, p)
        pass_on(2, p)
        pass_on(3, p)
    project_a(2)
    project_a(6)

    for cp in tt_copies:
        cp.wait()
    col = iota((128, 1024), 1)
    of_piece = 32 * (col // 32 % 4) + 4 * (col // 128) + 2 * (col // 16 % 2) + col // 4 % 2
    slot_of = mm(
        jnp.broadcast_to(slots_ref[...], (16, 128)).astype(BF16),
        (iota((128, 1024), 0) == of_piece).astype(BF16),
    ).astype(jnp.int32)
    row, col = iota((16, 1024), 0), iota((16, 1024), 1)
    chosen = (slot_of == 4 * c + row // 4) & (col % 4 == row % 4)
    every = turn_all[...].reshape(1024, HEAD)
    kind = col // 8 % 2
    ak_ref[...] = mm((chosen & (kind == 0)).astype(BF16), every).astype(BF16)
    av_ref[...] = mm((chosen & (kind == 1)).astype(BF16), every).astype(BF16)

    def rows_of(head):
        dy = (head + NY - y) % NY
        return pl.ds(pl.multiple_of(64 * jnp.where(dy >= 2, 5 - dy, dy), 64), 64)

    def share(total, sent, got, base):
        copies = []
        for d in (2, 3, 1):
            sent[d - 1] = total[rows_of((h + d) % NH)].astype(BF16)
            copies.append(send(sent.at[d - 1], got.at[3 - d], sem_h, base + 3 - d, dev(dh=d)))
        return copies

    def finish(total, got, copies, first):
        for cp in copies:
            cp.wait()
        whole = total[rows_of(h)]
        for j in range(3):
            whole = whole + got[j].astype(F32)
        for dx in range(NX):
            for j in range(4):
                at = 16 * (first + j) + 8 * ((x + dx) % NX)
                out_ref[pl.ds(pl.multiple_of(at, 8), 8)] = whole[
                    32 * dx + 8 * j : 32 * dx + 8 * j + 8
                ]

    for batch in range(1, 4):
        spread_arrived(batch)
        project_b(batch)
    to_b = share(sum_b, hb_send, hb_recv, 0)
    for p in range(4):
        passed(2, p)
    project_a(3)
    project_a(5)
    for p in range(4):
        passed(3, p)
    project_a(4)
    to_a = share(sum_a, ha_send, ha_recv, 3)
    finish(sum_b, hb_recv, to_b, 4)
    for cp in kv_copies + list(q_copies.values()) + list(a1.values()) + b1 + b2 + a2:
        cp.wait_send()
    finish(sum_a, ha_recv, to_a, 0)


def write_out(a_in, b_in, c_in, a_out, b_out, c_out, sems):
    pairs = ((a_in, a_out), (b_in, b_out), (c_in, c_out))
    copies = [pltpu.make_async_copy(src, dst, sems.at[i]) for i, (src, dst) in enumerate(pairs)]
    for cp in copies:
        cp.start()
    for cp in copies:
        cp.wait()


def on_device(
    queries, cache_keys, stored_cache_values, turn_keys, turn_values,
    block_mask, doc_ids, slot_ids, out_weight,
):
    anywhere = pl.BlockSpec(memory_space=pl.ANY)
    vmem = pl.BlockSpec(memory_space=pltpu.VMEM)
    sems = lambda n: pltpu.SemaphoreType.DMA((2, n))
    results = pl.pallas_call(
        kernel,
        out_shape=(
            jax.ShapeDtypeStruct((128, 256), F32),
            jax.ShapeDtypeStruct((16, HEAD), BF16),
            jax.ShapeDtypeStruct((16, HEAD), BF16),
        ),
        in_specs=[anywhere] * 9,
        out_specs=(vmem, vmem, vmem),
        scratch_shapes=[
            pltpu.VMEM((128, HEAD), BF16),
            pltpu.VMEM((NZ, 128, HEAD), BF16),
            pltpu.VMEM((NYX, KEYS, HEAD), BF16),
            pltpu.VMEM((NYX, KEYS, HEAD), BF16),
            pltpu.VMEM((4, 2 * KEYS, 2 * HEAD), BF16),
            pltpu.VMEM((2048, 256), BF16),
            pltpu.VMEM((NYX, 16, HEAD), BF16),
            pltpu.VMEM((NZ, NYX, 16, HEAD), BF16),
            pltpu.VMEM((ROWS, HEAD), BF16),
            pltpu.VMEM((ROWS, HEAD), BF16),
            pltpu.VMEM((NY, 128), jnp.int32),
            pltpu.VMEM((1, 128), jnp.int32),
            pltpu.SMEM((NY, 128), jnp.int32),
            pltpu.VMEM((4, 256, 128), F32),
            pltpu.VMEM((4, 256, 256), F32),
            pltpu.VMEM((NZ, NZ, 16, HEAD), BF16),
            pltpu.VMEM((2 * NZ, 128), F32),
            pltpu.VMEM((NZ, NZ, 16, HEAD), BF16),
            pltpu.VMEM((NZ, 2 * NZ, 128), F32),
            pltpu.VMEM((128, 128), F32),
            pltpu.VMEM((NZ, NYX, 32, 256), BF16),
            pltpu.VMEM((NZ, NYX, 32, 256), BF16),
            pltpu.VMEM((256, 256), F32),
            pltpu.VMEM((256, 256), F32),
            pltpu.VMEM((3, 64, 256), BF16),
            pltpu.VMEM((3, 64, 256), BF16),
            pltpu.VMEM((3, 64, 256), BF16),
            pltpu.VMEM((3, 64, 256), BF16),
            pltpu.SemaphoreType.DMA((9,)),
            sems(8), sems(16), sems(8), sems(8), sems(8), sems(24), sems(8), sems(8), sems(32), sems(32), sems(6),
        ],
        compiler_params=pltpu.CompilerParams(
            collective_id=0, has_side_effects=True, vmem_limit_bytes=60 * 1024 * 1024
        ),
        name="turn_attention",
    )(
        queries.reshape(128, HEAD),
        cache_keys.reshape(KEYS, HEAD),
        stored_cache_values.reshape(KEYS, HEAD),
        out_weight,
        turn_keys.reshape(ROWS, HEAD),
        turn_values.reshape(ROWS, HEAD),
        doc_ids.reshape(NY, 128),
        slot_ids.reshape(1, 128),
        block_mask,
    )
    layer_out, append_keys, append_values = pl.pallas_call(
        write_out,
        out_shape=tuple(jax.ShapeDtypeStruct(r.shape, r.dtype) for r in results),
        in_specs=[anywhere] * 3,
        out_specs=(anywhere,) * 3,
        scratch_shapes=[pltpu.SemaphoreType.DMA((3,))],
        compiler_params=pltpu.CompilerParams(vmem_limit_bytes=60 * 1024 * 1024),
        name="write_out",
    )(*results)
    return (
        layer_out,
        append_keys.reshape(16, 1, HEAD),
        append_values.reshape(16, 1, HEAD),
    )


def solution(mesh):
    placed = (
        P("ctx", "head", None),
        P("ctx", "head", None),
        P("ctx", "head", None),
        P("ctx", "head", None),
        P("ctx", "head", None),
        P(),
        P(),
        P(),
        P("head", "ctx"),
    )
    return jax.shard_map(
        on_device,
        mesh=mesh,
        in_specs=placed,
        out_specs=(P("head", "ctx"), P("ctx", "head", None), P("ctx", "head", None)),
        check_vma=False,
    )
```

```python
import math

import jax
import jax.numpy as jnp
from jax import lax
from jax.experimental import pallas as pl
from jax.experimental.pallas import tpu as pltpu
from jax.sharding import PartitionSpec as P

MESH = pl.DeviceIdType.MESH
F32 = jnp.float32
BF16 = jnp.bfloat16

NY, NZ, NX = 4, 8, 2
NYX = NY * NX
NH = 4
HEAD = 128
KEYS = 256
GROUP = 16
ROWS = 8
NEG = -1e30
FLOOR = -1e29
SCALE = math.log2(math.e) / math.sqrt(HEAD)

YX = [(0, 0), (0, 1), (1, 0), (1, 1), (3, 0), (3, 1), (2, 0), (2, 1)]
YX_ORDER = [1, 2, 4, 3, 5, 6, 7]
YS = [0, 1, 3, 2]
ZS = [0, 1, 7, 2, 6, 3, 5, 4]
Z_ORDER = [1, 7, 2, 6, 3, 5, 4]
Z_BATCHES = [(0, 1), (1, 3), (3, 5), (5, 8)]
NA = 4
RA, RB = NA * ROWS, (NZ - NA) * ROWS
DIRECT = True
W_PARTS = 4
KEY_GROUPS = [(0, 1), (2, 4), (6, 3), (5, 7)]
BLOCKS = [
    (0, 0), (0, 1), (1, 0), (1, 1), (0, 2), (1, 2), (2, 0), (2, 1), (2, 2), (0, 3), (1, 3), (2, 3),
    (3, 0), (3, 1), (3, 2), (3, 3),
]


def nt(a, b):
    return lax.dot_general(a, b, (((1,), (1,)), ((), ())), preferred_element_type=F32)


def mm(a, b):
    return jnp.dot(a, b, preferred_element_type=F32)


def iota(shape, dim):
    return lax.broadcasted_iota(jnp.int32, shape, dim)


def back_yx(r):
    dy, dx = YX[r]
    return YX.index(((NY - dy) % NY, dx))


def kernel(
    q_in, ck_in, cv_in, w_in, tk_in, tv_in, doc_in, slot_in, mask_in,
    out_ref, ak_ref, av_ref,
    q_raw, q_all, k_all, v_all, v_wide, w_all, turn_yx, turn_all, tk, tv, docs_ref, slots_ref, mask_ref,
    peak, acc, o_send, st_send, o_recv, st_recv, factors, part_a, part_b, sum_a, sum_b,
    ha_send, ha_recv, hb_send, hb_recv,
    sem_in, sem_w, sem_q, sem_kv, sem_t, sem_tz, sem_tt, sem_rs, sem_a1, sem_b1, sem_a2, sem_b2, sem_h,
):
    c = lax.axis_index("ctx")
    h = lax.axis_index("head")
    y, z, x = c // (NZ * NX), (c // NX) % NZ, c % NX
    yx = y * NX + x

    def dev(dy=0, dz=0, dx=0, dh=0):
        ty, tz, tx = (y + dy) % NY, (z + dz) % NZ, (x + dx) % NX
        return ((ty * NZ + tz) * NX + tx, (h + dh) % NH)

    def to_y(i):
        return dev(dy=YS[i])

    def back_y(i):
        return YS.index((NY - YS[i]) % NY)

    def to_yx(r):
        return dev(dy=YX[r][0], dx=YX[r][1])

    def send(src, dst, sems, i, device):
        copy = pltpu.make_async_remote_copy(
            src_ref=src, dst_ref=dst, send_sem=sems.at[0, i], recv_sem=sems.at[1, i],
            device_id=device, device_id_type=MESH,
        )
        copy.start()
        return copy

    def arrived(ref, sems, i):
        pltpu.make_async_copy(ref, ref, sems.at[1, i]).wait()

    def fetch(src, dst, i):
        copy = pltpu.make_async_copy(src, dst, sem_in.at[i])
        copy.start()
        return copy

    barrier = pltpu.get_barrier_semaphore()
    peers = [to_yx(r) for r in YX_ORDER] + [dev(dz=d) for d in Z_ORDER]
    peers += [dev(dx=dx, dh=d) for dx in range(NX) for d in range(1, NH)]
    for p in peers:
        pl.semaphore_signal(barrier, inc=1, device_id=p, device_id_type=MESH)

    get_q = fetch(q_in, q_raw, 0)
    get_small = [
        fetch(tk_in, tk, 1), fetch(tv_in, tv, 2), fetch(doc_in, docs_ref, 3),
        fetch(slot_in, slots_ref, 4), fetch(mask_in, mask_ref, 5),
    ]
    get_kv = [fetch(ck_in, k_all.at[0], 6), fetch(cv_in, v_all.at[0], 7)]
    get_w = fetch(w_in, w_all.at[0], 8)

    pl.semaphore_wait(barrier, len(peers))

    def give_k(src, slot, device):
        return send(src, k_all.at[slot], sem_kv, 2 * slot, device)

    def give_v(src, slot, device):
        return send(src, v_all.at[slot], sem_kv, 2 * slot + 1, device)

    kv_copies = [give_v(cv_in, 1, to_yx(1))]
    for r in (2, 4, 6):
        kv_copies.append(give_k(ck_in, back_yx(r), to_yx(r)))
    kv_copies.append(give_k(ck_in, 1, to_yx(1)))
    for r in (2, 4, 6):
        kv_copies.append(give_v(cv_in, back_yx(r), to_yx(r)))

    get_q.wait()
    i0, i1 = iota((128, 128), 0), iota((128, 128), 1)
    order = (i1 == (i0 % ROWS) * GROUP + i0 // ROWS).astype(BF16)
    q_all[0] = mm(order, q_raw[...]).astype(BF16)
    q_copies = {d: send(q_all.at[0], q_all.at[ZS.index(NZ - d)], sem_q, ZS.index(NZ - d), dev(dz=d)) for d in Z_ORDER}
    for cp in get_small:
        cp.wait()
    mine = jnp.concatenate([tk[...].astype(F32), tv[...].astype(F32)], axis=0).astype(BF16)
    turn_yx[yx] = mine
    turn_all[z, yx] = mine
    t_copies = [send(turn_yx.at[yx], turn_yx.at[yx], sem_t, r, to_yx(r)) for r in YX_ORDER]
    tz_copies = [send(turn_yx.at[yx], turn_all.at[z, yx], sem_tz, d, dev(dz=d)) for d in Z_ORDER]

    docs = docs_ref[...]
    key_token = 16 * z + 8 * (i1 // 16 % 2) + i1 % 8
    by_y = mm(
        jnp.concatenate([docs.astype(F32), jnp.zeros((12, 128), F32)], axis=0).astype(BF16),
        (i0 == key_token).astype(BF16),
    )
    key_doc = jnp.sum(
        jnp.where(iota((16, 128), 0) == iota((16, 128), 1) // 32, by_y, 0.0), axis=0, keepdims=True
    )
    doc_mine = jnp.sum(
        jnp.where(iota((NY, 128), 0) == y, docs, 0), axis=0, keepdims=True
    ).astype(F32)
    right_key = (i1 // 8 % 2 == 0)

    def sight(slot):
        query_token = 16 * ((z + ZS[slot]) % NZ) + 8 * x + i0 % 8
        query_doc = jnp.sum(jnp.where(i1 == query_token, doc_mine, 0.0), axis=1, keepdims=True)
        see = (
            (128 * (i1 // 32) + key_token <= 128 * y + query_token)
            & (key_doc == query_doc)
            & right_key
        )
        return jnp.where(see, 0.0, NEG)

    diagonal = i0 == i1

    arrived(v_all.at[1], sem_kv, 3)
    for r in (2, 4, 6):
        kv_copies.append(give_v(v_all.at[1], back_yx(r + 1), to_yx(r)))
    for r in (2, 4, 6):
        arrived(k_all.at[r], sem_kv, 2 * r)
        kv_copies.append(give_k(k_all.at[r], r + 1, to_yx(1)))
    w_rows = 2048 // W_PARTS
    w_copies = []
    for i in range(W_PARTS):
        rows = pl.ds(w_rows * i, w_rows)
        w_copies.append(send(w_in.at[rows], w_all.at[1, rows], sem_w, i, dev(dx=1)))

    have = {("k", 2), ("k", 4), ("k", 6), ("v", 1)}
    biases = {}
    for g, i in BLOCKS:
        last = g == 3
        if i == 0:
            for j, r in enumerate(KEY_GROUPS[g]):
                if r == 0:
                    for cp in get_kv:
                        cp.wait()
                else:
                    if ("k", r) not in have:
                        arrived(k_all.at[r], sem_kv, 2 * r)
                    if ("v", r) not in have:
                        arrived(v_all.at[r], sem_kv, 2 * r + 1)
                v_wide[g, KEYS * j : KEYS * (j + 1), :HEAD] = v_all[r]
            v_wide[g, :, HEAD:] = jnp.ones((2 * KEYS, HEAD), BF16)
            biases[g] = []
            for r in KEY_GROUPS[g]:
                source = ((y + YX[r][0]) % NY * NZ + z) * NX + (x + YX[r][1]) % NX
                for b in range(2):
                    biases[g].append(jnp.where(mask_ref[y, 2 * source + b] == 1, 0.0, NEG))
            if last:
                for cp in t_copies:
                    cp.wait()
                fresh = turn_yx[...].reshape(128, HEAD)
                fresh_v = mm((i1 == i0 + 8).astype(BF16), fresh).astype(BF16)
                fresh_v = jnp.concatenate([fresh_v, jnp.ones((128, HEAD), BF16)], axis=1)
        if g == 0:
            for slot in (2 * i, 2 * i + 1):
                if slot:
                    arrived(q_all.at[slot], sem_q, slot)
        q = q_all[2 * i : 2 * i + 2].reshape(256, HEAD)
        parts = []
        for j, r in enumerate(KEY_GROUPS[g]):
            s = nt(q, k_all[r])
            parts += [
                s[:, :128] * SCALE + biases[g][2 * j], s[:, 128:] * SCALE + biases[g][2 * j + 1]
            ]
        values = v_wide[g]
        if last:
            see = jnp.concatenate([sight(2 * i), sight(2 * i + 1)], axis=0)
            parts.append(nt(q, fresh) * SCALE + see)
            values = jnp.concatenate([values, fresh_v], axis=0)
        top = parts[0]
        for p in parts[1:]:
            top = jnp.maximum(top, p)
        top = jnp.broadcast_to(jnp.max(top, axis=1, keepdims=True), (256, 128))
        old = FLOOR if g == 0 else peak[i]
        top = jnp.maximum(top, old)
        p = jnp.concatenate([jnp.exp2(p - top).astype(BF16) for p in parts], axis=1)
        o = mm(p, values)
        if g > 0:
            keep = jnp.exp2(old - top)
            o = o + acc[i] * jnp.concatenate([keep, keep], axis=1)
        if not last:
            acc[i] = o
            peak[i] = top
            continue
        for j in range(2):
            rows = slice(128 * j, 128 * (j + 1))
            of = (z + ZS[2 * i + j]) % NZ
            o_send[:, of] = o[rows, :HEAD].astype(BF16).reshape(NZ, 16, HEAD)
            st_send[pl.ds(of, 1)] = jnp.sum(
                jnp.where(diagonal, top[rows], 0.0), axis=0, keepdims=True
            )
            st_send[pl.ds(NZ + of, 1)] = jnp.sum(
                jnp.where(diagonal, o[rows, HEAD:], 0.0), axis=0, keepdims=True
            )

    halves = (pl.ds(0, NA), pl.ds(NA, NZ - NA))
    rs = [[], []]
    for d in Z_ORDER:
        rs[0].append(send(st_send, st_recv.at[z], sem_rs, d, dev(dz=d)))
    for half in range(2):
        for d in Z_ORDER:
            rs[half].append(
                send(
                    o_send.at[(z + d) % NZ, halves[half]], o_recv.at[z, halves[half]],
                    sem_rs, 8 * (half + 1) + d, dev(dz=d),
                )
            )
    o_recv[z] = o_send[z]
    st_recv[z] = st_send[...]
    for cp in tz_copies:
        cp.wait()
    tt_copies = [send(turn_all.at[:, yx], turn_all.at[:, yx], sem_tt, r, to_yx(r)) for r in YX_ORDER]
    for cp in rs[0]:
        cp.wait()
    peaks, totals = st_recv[:, :NZ], st_recv[:, NZ:]
    factor = jnp.exp2(peaks - jnp.max(peaks, axis=0, keepdims=True))
    factor = factor / jnp.sum(factor * totals, axis=0, keepdims=True)
    factors[...] = jnp.concatenate(
        [factor.reshape(NZ * NZ, 128), jnp.zeros((128 - NZ * NZ, 128), F32)], axis=0
    ).T
    factor = factors[pl.ds(pl.multiple_of(16 * z, 16), 16)]

    def attended(half):
        out = []
        for of in (range(NA), range(NA, NZ))[half]:
            num = 0.0
            for j in range(NZ):
                at = NZ * j + of
                num = num + factor[:, at : at + 1] * o_recv[j, of].astype(F32)
            out.append(jnp.concatenate([num[:ROWS], num[ROWS:]], axis=1))
        return jnp.concatenate(out, axis=0).astype(BF16)

    part_a[0, 0] = attended(0)
    a1 = [
        send(part_a.at[0, 0], part_a.at[0, back_y(i)], sem_a1, back_y(i), to_y(i)) for i in (1, 2, 3)
    ]
    a2, b2 = [], []

    def give(slot, i, steps):
        for step in steps:
            dst = (slot - step) % NZ
            if dst != 4 or (step > 0) == (i < NY // 2):
                a2.append(
                    send(part_a.at[slot, i], part_a.at[dst, i], sem_a2, NZ * i + dst, dev(dz=step))
                )

    def got(slot, i):
        arrived(part_a.at[slot, i], sem_a2, NZ * i + slot)

    give(0, 0, (1, -1, 2, -2))
    for cp in rs[1]:
        cp.wait()
    part_b[0, 0] = attended(1)
    b1 = [
        send(part_b.at[0, 0], part_b.at[ZS.index(NZ - d), 0], sem_b1, ZS.index(NZ - d), dev(dz=d))
        for d in Z_ORDER
    ]

    def spread(batch):
        lo, hi = Z_BATCHES[batch]
        for s in range(lo, hi):
            if s:
                arrived(part_b.at[s, 0], sem_b1, s)
        for i in (1, 2, 3):
            b = back_y(i)
            b2.append(
                send(
                    part_b.at[pl.ds(lo, hi - lo), 0], part_b.at[pl.ds(lo, hi - lo), b],
                    sem_b2, 4 * batch + b, to_y(i),
                )
            )

    def spread_arrived(batch):
        lo, hi = Z_BATCHES[batch]
        for i in (1, 2, 3):
            arrived(part_b.at[pl.ds(lo, hi - lo), i], sem_b2, 4 * batch + i)

    def project(part, total, slot, dz, columns):
        at = pl.multiple_of((z + dz) % NZ * 256, 256)
        size = part.shape[1] * part.shape[2]
        new = mm(part[slot].reshape(size, 256), w_all[columns, pl.ds(at, 256)])
        total[columns] = new if dz == 0 else total[columns] + new

    def project_a(slots, columns):
        for slot in slots:
            project(part_a, sum_a, slot, slot, columns)

    def project_b(batches, columns):
        for batch in batches:
            for s in range(*Z_BATCHES[batch]):
                project(part_b, sum_b, s, ZS[s], columns)

    spread(0)
    for i in (1, 2, 3):
        arrived(part_a.at[0, i], sem_a1, i)
        give(0, i, (1, -1, 2, -2))
        if i == 2:
            spread(1)
    spread(2)
    get_w.wait()
    project_a((0,), 0)
    for i in range(NY):
        got(6, i)
        give(6, i, (1, 2))
        got(2, i)
        give(2, i, (-1, -2))
        if i == 0:
            spread(3)
        got(1, i)
        got(7, i)
    project_a((1, 7, 2, 6), 0)
    for batch in range(3):
        spread_arrived(batch)
        project_b((batch,), 0)

    for cp in tt_copies:
        cp.wait()
    col = iota((128, 1024), 1)
    of_piece = 32 * (col // 32 % 4) + 4 * (col // 128) + 2 * (col // 16 % 2) + col // 4 % 2
    slot_of = mm(
        jnp.broadcast_to(slots_ref[...], (16, 128)).astype(BF16),
        (iota((128, 1024), 0) == of_piece).astype(BF16),
    ).astype(jnp.int32)
    row, col = iota((16, 1024), 0), iota((16, 1024), 1)
    chosen = (slot_of == 4 * c + row // 4) & (col % 4 == row % 4)
    every = turn_all[...].reshape(1024, HEAD)
    kind = col // 8 % 2
    ak_ref[...] = mm((chosen & (kind == 0)).astype(BF16), every).astype(BF16)
    av_ref[...] = mm((chosen & (kind == 1)).astype(BF16), every).astype(BF16)

    for cp in w_copies:
        cp.wait()
    project_a((0, 1, 7, 2, 6), 1)
    project_b((0, 1, 2), 1)

    def rows_of(head, size):
        dy = (head + NY - y) % NY
        return pl.ds(pl.multiple_of(size * jnp.where(dy >= 2, 5 - dy, dy), size), size)

    def share(total, sent, got, base, size):
        copies = []
        for columns, d in ((0, 2), (1, 2), (0, 3), (1, 3), (0, 1), (1, 1), (1, 0)):
            slot = NH * columns + d
            back = NH * columns + (NH - d) % NH
            sent[slot] = total[columns, rows_of((h + d) % NH, size)].astype(BF16)
            copies.append(
                send(sent.at[slot], got.at[back], sem_h, base + back, dev(dx=columns, dh=d))
            )
        return copies

    def finish(total, got, copies, first, size):
        for cp in copies:
            cp.wait()
        whole = [total[0, rows_of(h, size)], got[NH].astype(F32)]
        for columns in range(2):
            for d in range(1, NH):
                whole[columns] = whole[columns] + got[NH * columns + d].astype(F32)
            for j in range(size // ROWS):
                at = 16 * (first + j) + 8 * ((x + columns) % NX)
                out_ref[pl.ds(pl.multiple_of(at, 8), 8)] = whole[columns][8 * j : 8 * j + 8]

    spread_arrived(3)
    project_b((3,), 0)
    project_b((3,), 1)
    to_b = share(sum_b, hb_send, hb_recv, 0, RB)
    for slot in (3, 5, 4):
        for i in range(NY):
            got(slot, i)
        project_a((slot,), 0)
        project_a((slot,), 1)
    to_a = share(sum_a, ha_send, ha_recv, 8, RA)
    finish(sum_b, hb_recv, to_b, NA, RB)
    for cp in kv_copies + list(q_copies.values()) + a1 + b1 + b2 + a2:
        cp.wait_send()
    finish(sum_a, ha_recv, to_a, 0, RA)


def write_out(a_in, b_in, c_in, a_out, b_out, c_out, a_mid, b_mid, c_mid, sems):
    ins = [(a_in, a_mid), (b_in, b_mid), (c_in, c_mid)]
    outs = [(a_mid, a_out), (b_mid, b_out), (c_mid, c_out)]
    ins = [pltpu.make_async_copy(*pair, sems.at[0, i]) for i, pair in enumerate(ins)]
    outs = [pltpu.make_async_copy(*pair, sems.at[1, i]) for i, pair in enumerate(outs)]
    for cp in ins:
        cp.start()
    for i in (1, 2, 0):
        ins[i].wait()
        outs[i].start()
    for cp in outs:
        cp.wait()


def on_device(
    queries, cache_keys, stored_cache_values, turn_keys, turn_values,
    block_mask, doc_ids, slot_ids, out_weight,
):
    anywhere = pl.BlockSpec(memory_space=pl.ANY)
    vmem = pl.BlockSpec(memory_space=pltpu.VMEM)
    sems = lambda n: pltpu.SemaphoreType.DMA((2, n))
    results = pl.pallas_call(
        kernel,
        out_shape=(
            jax.ShapeDtypeStruct((128, 256), F32),
            jax.ShapeDtypeStruct((16, HEAD), BF16),
            jax.ShapeDtypeStruct((16, HEAD), BF16),
        ),
        in_specs=[anywhere] * 9,
        out_specs=(vmem, vmem, vmem),
        scratch_shapes=[
            pltpu.VMEM((128, HEAD), BF16),
            pltpu.VMEM((NZ, 128, HEAD), BF16),
            pltpu.VMEM((NYX, KEYS, HEAD), BF16),
            pltpu.VMEM((NYX, KEYS, HEAD), BF16),
            pltpu.VMEM((4, 2 * KEYS, 2 * HEAD), BF16),
            pltpu.VMEM((NX, 2048, 256), BF16),
            pltpu.VMEM((NYX, 16, HEAD), BF16),
            pltpu.VMEM((NZ, NYX, 16, HEAD), BF16),
            pltpu.VMEM((ROWS, HEAD), BF16),
            pltpu.VMEM((ROWS, HEAD), BF16),
            pltpu.VMEM((NY, 128), jnp.int32),
            pltpu.VMEM((1, 128), jnp.int32),
            pltpu.SMEM((NY, 128), jnp.int32),
            pltpu.VMEM((4, 256, 128), F32),
            pltpu.VMEM((4, 256, 256), F32),
            pltpu.VMEM((NZ, NZ, 16, HEAD), BF16),
            pltpu.VMEM((2 * NZ, 128), F32),
            pltpu.VMEM((NZ, NZ, 16, HEAD), BF16),
            pltpu.VMEM((NZ, 2 * NZ, 128), F32),
            pltpu.VMEM((128, 128), F32),
            pltpu.VMEM((NZ, NY, RA, 256), BF16),
            pltpu.VMEM((NZ, NY, RB, 256), BF16),
            pltpu.VMEM((NX, NY * RA, 256), F32),
            pltpu.VMEM((NX, NY * RB, 256), F32),
            pltpu.VMEM((2 * NH, RA, 256), BF16),
            pltpu.VMEM((2 * NH, RA, 256), BF16),
            pltpu.VMEM((2 * NH, RB, 256), BF16),
            pltpu.VMEM((2 * NH, RB, 256), BF16),
            pltpu.SemaphoreType.DMA((9,)),
            sems(W_PARTS), sems(8), sems(16), sems(8), sems(8), sems(8), sems(24), sems(4), sems(8), sems(32),
            sems(16), sems(16),
        ],
        compiler_params=pltpu.CompilerParams(
            collective_id=0, has_side_effects=True, vmem_limit_bytes=60 * 1024 * 1024
        ),
        name="turn_attention",
    )(
        queries.reshape(128, HEAD),
        cache_keys.reshape(KEYS, HEAD),
        stored_cache_values.reshape(KEYS, HEAD),
        out_weight,
        turn_keys.reshape(ROWS, HEAD),
        turn_values.reshape(ROWS, HEAD),
        doc_ids.reshape(NY, 128),
        slot_ids.reshape(1, 128),
        block_mask,
    )
    layer_out, append_keys, append_values = pl.pallas_call(
        write_out,
        out_shape=tuple(jax.ShapeDtypeStruct(r.shape, r.dtype) for r in results),
        in_specs=[anywhere] * 3,
        out_specs=(anywhere,) * 3,
        scratch_shapes=[pltpu.VMEM(r.shape, r.dtype) for r in results]
        + [pltpu.SemaphoreType.DMA((2, 3))],
        compiler_params=pltpu.CompilerParams(vmem_limit_bytes=60 * 1024 * 1024),
        name="write_out",
    )(*results)
    return (
        layer_out,
        append_keys.reshape(16, 1, HEAD),
        append_values.reshape(16, 1, HEAD),
    )


def solution(mesh):
    placed = (
        P("ctx", "head", None),
        P("ctx", "head", None),
        P("ctx", "head", None),
        P("ctx", "head", None),
        P("ctx", "head", None),
        P(),
        P(),
        P(),
        P("head", "ctx"),
    )
    return jax.shard_map(
        on_device,
        mesh=mesh,
        in_specs=placed,
        out_specs=(P("head", "ctx"), P("ctx", "head", None), P("ctx", "head", None)),
        check_vma=False,
    )
```

```python
import math

import jax
import jax.numpy as jnp
from jax import lax
from jax.experimental import pallas as pl
from jax.experimental.pallas import tpu as pltpu
from jax.sharding import PartitionSpec as P

MESH = pl.DeviceIdType.MESH
F32 = jnp.float32
BF16 = jnp.bfloat16

NY, NZ, NX = 4, 8, 2
NYX = NY * NX
NH = 4
HEAD = 128
KEYS = 256
GROUP = 16
ROWS = 8
NEG = -1e30
FLOOR = -1e29
SCALE = math.log2(math.e) / math.sqrt(HEAD)

YX = [(0, 0), (0, 1), (1, 0), (1, 1), (3, 0), (3, 1), (2, 0), (2, 1)]
YX_ORDER = [1, 2, 4, 3, 5, 6, 7]
YS = [0, 1, 3, 2]
ZS = [0, 1, 7, 2, 6, 3, 5, 4]
Z_ORDER = [1, 7, 2, 6, 3, 5, 4]
Z_BATCHES = [(0, 1), (1, 3), (3, 5), (5, 7), (7, 8)]
NA = 4
RA, RB = NA * ROWS, (NZ - NA) * ROWS
DIRECT = True
SENT = [
    "q", "k", "v", "t", "tz", "tt", "st", "rs0", "rs1", "a1", "b1", "a2", "b2", "ha", "hb", "w",
]
GOT = [
    "q0", "q1", "q2", "q3", "v1", "k1", "k2", "k4", "k6", "g1", "g2", "g3", "t", "tz", "tt", "st",
    "rs0", "rs1", "a1_1", "a1_2", "a1_3", "b1_1", "b1_2", "b1_3", "b1_4", "a2_0", "a2_1", "a2_2",
    "a2_3", "a2_side", "a2_far", "b2_0", "b2_1", "b2_2", "b2_3", "b2_4", "ha", "hb", "w",
]
KEY_GROUPS = [(0, 1), (2, 4), (6, 3), (5, 7)]
BLOCKS = [
    (0, 0), (0, 1), (1, 0), (1, 1), (0, 2), (1, 2), (2, 0), (2, 1), (2, 2), (0, 3), (1, 3), (2, 3),
    (3, 0), (3, 1), (3, 2), (3, 3),
]


def nt(a, b):
    return lax.dot_general(a, b, (((1,), (1,)), ((), ())), preferred_element_type=F32)


def mm(a, b):
    return jnp.dot(a, b, preferred_element_type=F32)


def iota(shape, dim):
    return lax.broadcasted_iota(jnp.int32, shape, dim)


def back_yx(r):
    dy, dx = YX[r]
    return YX.index(((NY - dy) % NY, dx))


def kernel(
    q_in, ck_in, cv_in, w_in, tk_in, tv_in, doc_in, slot_in, mask_in,
    out_hbm, ak_hbm, av_hbm,
    q_raw, q_all, k_all, v_all, v_wide, w_all, turn_yx, turn_all, tk, tv, docs_ref, slots_ref, mask_ref,
    peak, acc, o_send, st_send, o_recv, st_recv, factors, wide, sights, part_a, part_b, sum_a, sum_b,
    ha_send, ha_recv, hb_send, hb_recv, out_ref, ak_ref, av_ref,
    sem_in, sem_out, sem_sent, sem_got,
):
    c = lax.axis_index("ctx")
    h = lax.axis_index("head")
    y, z, x = c // (NZ * NX), (c // NX) % NZ, c % NX
    yx = y * NX + x

    def dev(dy=0, dz=0, dx=0, dh=0):
        ty, tz, tx = (y + dy) % NY, (z + dz) % NZ, (x + dx) % NX
        return ((ty * NZ + tz) * NX + tx, (h + dh) % NH)

    def to_y(i):
        return dev(dy=YS[i])

    def back_y(i):
        return YS.index((NY - YS[i]) % NY)

    def to_yx(r):
        return dev(dy=YX[r][0], dx=YX[r][1])

    def send(src, dst, sent, got, device):
        pltpu.make_async_remote_copy(
            src_ref=src, dst_ref=dst, send_sem=sem_sent.at[SENT.index(sent)],
            recv_sem=sem_got.at[GOT.index(got)], device_id=device, device_id_type=MESH,
        ).start()

    def arrived(ref, got):
        pltpu.make_async_copy(ref, ref, sem_got.at[GOT.index(got)]).wait()

    def left(ref, sent):
        pltpu.make_async_copy(ref, ref, sem_sent.at[SENT.index(sent)]).wait()

    def put(src, dst, i):
        copy = pltpu.make_async_copy(src, dst, sem_out.at[i])
        copy.start()
        return copy

    def fetch(src, dst, i):
        copy = pltpu.make_async_copy(src, dst, sem_in.at[i])
        copy.start()
        return copy

    barrier = pltpu.get_barrier_semaphore()
    peers = [to_yx(r) for r in YX_ORDER] + [dev(dz=d) for d in Z_ORDER]
    peers += [dev(dx=dx, dh=d) for dx in range(NX) for d in range(1, NH)]
    for p in peers:
        pl.semaphore_signal(barrier, inc=1, device_id=p, device_id_type=MESH)

    get_q = fetch(q_in, q_raw, 0)
    get_small = [
        fetch(tk_in, tk, 1), fetch(tv_in, tv, 2), fetch(doc_in, docs_ref, 3),
        fetch(slot_in, slots_ref, 4), fetch(mask_in, mask_ref, 5),
    ]
    get_kv = [fetch(ck_in, k_all.at[0], 6), fetch(cv_in, v_all.at[0], 7)]
    get_w = fetch(w_in, w_all.at[0], 8)

    pl.semaphore_wait(barrier, len(peers))

    def give_k(src, slot, device):
        got = f"k{slot}" if slot in (1, 2, 4, 6) else ("g2" if slot == 3 else "g3")
        send(src, k_all.at[slot], "k", got, device)

    def give_v(src, slot, device):
        got = {1: "v1", 2: "g1", 4: "g1", 3: "g2", 6: "g2"}.get(slot, "g3")
        send(src, v_all.at[slot], "v", got, device)

    give_v(cv_in, 1, to_yx(1))
    for r in (2, 4, 6):
        give_k(ck_in, back_yx(r), to_yx(r))
    give_k(ck_in, 1, to_yx(1))
    for r in (2, 4, 6):
        give_v(cv_in, back_yx(r), to_yx(r))

    get_q.wait()
    i0, i1 = iota((128, 128), 0), iota((128, 128), 1)
    order = (i1 == (i0 % ROWS) * GROUP + i0 // ROWS).astype(BF16)
    q_all[0] = mm(order, q_raw[...]).astype(BF16)
    for d in Z_ORDER:
        slot = ZS.index(NZ - d)
        send(q_all.at[0], q_all.at[slot], "q", f"q{slot // 2}", dev(dz=d))
    for cp in get_small:
        cp.wait()
    mine = jnp.concatenate([tk[...].astype(F32), tv[...].astype(F32)], axis=0).astype(BF16)
    turn_yx[yx] = mine
    turn_all[z, yx] = mine
    for r in YX_ORDER:
        send(turn_yx.at[yx], turn_yx.at[yx], "t", "t", to_yx(r))
    for d in Z_ORDER:
        send(turn_yx.at[yx], turn_all.at[z, yx], "tz", "tz", dev(dz=d))

    docs = docs_ref[...]
    key_token = 16 * z + 8 * (i1 // 16 % 2) + i1 % 8
    by_y = mm(
        jnp.concatenate([docs.astype(F32), jnp.zeros((12, 128), F32)], axis=0).astype(BF16),
        (i0 == key_token).astype(BF16),
    )
    key_doc = jnp.sum(
        jnp.where(iota((16, 128), 0) == iota((16, 128), 1) // 32, by_y, 0.0), axis=0, keepdims=True
    )
    doc_mine = jnp.sum(
        jnp.where(iota((NY, 128), 0) == y, docs, 0), axis=0, keepdims=True
    ).astype(F32)
    right_key = (i1 // 8 % 2 == 0)

    def sight(slot):
        query_token = 16 * ((z + ZS[slot]) % NZ) + 8 * x + i0 % 8
        query_doc = jnp.sum(jnp.where(i1 == query_token, doc_mine, 0.0), axis=1, keepdims=True)
        see = (
            (128 * (i1 // 32) + key_token <= 128 * y + query_token)
            & (key_doc == query_doc)
            & right_key
        )
        return jnp.where(see, 0.0, NEG)

    diagonal = i0 == i1

    arrived(v_all.at[1], "v1")
    for r in (2, 4, 6):
        give_v(v_all.at[1], back_yx(r + 1), to_yx(r))
    for slot in range(NZ):
        sights[slot] = sight(slot)
    for r in (2, 4, 6):
        arrived(k_all.at[r], f"k{r}")
        give_k(k_all.at[r], r + 1, to_yx(1))
    send(w_in, w_all.at[1], "w", "w", dev(dx=1))

    biases = {}
    for g, i in BLOCKS:
        last = g == 3
        if i == 0:
            if g == 0:
                for cp in get_kv:
                    cp.wait()
                arrived(k_all.at[1], "k1")
            else:
                arrived(k_all.at[pl.ds(0, g + 1)], f"g{g}")
            for j, r in enumerate(KEY_GROUPS[g]):
                v_wide[g, KEYS * j : KEYS * (j + 1), :HEAD] = v_all[r]
            v_wide[g, :, HEAD:] = jnp.ones((2 * KEYS, HEAD), BF16)
            biases[g] = []
            for r in KEY_GROUPS[g]:
                source = ((y + YX[r][0]) % NY * NZ + z) * NX + (x + YX[r][1]) % NX
                for b in range(2):
                    biases[g].append(jnp.where(mask_ref[y, 2 * source + b] == 1, 0.0, NEG))
            if g == 1:
                arrived(turn_yx.at[pl.ds(1, NYX - 1)], "t")
                fresh = turn_yx[...].reshape(128, HEAD)
                fresh_v = mm((i1 == i0 + 8).astype(BF16), fresh).astype(BF16)
                fresh_v = jnp.concatenate([fresh_v, jnp.ones((128, HEAD), BF16)], axis=1)
        if g == 0:
            arrived(q_all.at[pl.ds(2 * i, 2)] if i else q_all.at[1], f"q{i}")
        q = q_all[2 * i : 2 * i + 2].reshape(256, HEAD)
        parts = []
        for j, r in enumerate(KEY_GROUPS[g]):
            s = nt(q, k_all[r])
            parts += [
                s[:, :128] * SCALE + biases[g][2 * j], s[:, 128:] * SCALE + biases[g][2 * j + 1]
            ]
        values = v_wide[g]
        if g == 1:
            parts.append(nt(q, fresh) * SCALE + sights[2 * i : 2 * i + 2].reshape(256, 128))
            values = jnp.concatenate([values, fresh_v], axis=0)
        top = parts[0]
        for p in parts[1:]:
            top = jnp.maximum(top, p)
        top = jnp.broadcast_to(jnp.max(top, axis=1, keepdims=True), (256, 128))
        old = FLOOR if g == 0 else peak[i]
        top = jnp.maximum(top, old)
        p = jnp.concatenate([jnp.exp2(p - top).astype(BF16) for p in parts], axis=1)
        o = mm(p, values)
        if g > 0:
            keep = jnp.exp2(old - top)
            o = o + acc[i] * jnp.concatenate([keep, keep], axis=1)
        if not last:
            acc[i] = o
            peak[i] = top
            continue
        for j in range(2):
            rows = slice(128 * j, 128 * (j + 1))
            of = (z + ZS[2 * i + j]) % NZ
            o_send[:, of] = o[rows, :HEAD].astype(BF16).reshape(NZ, 16, HEAD)
            st_send[pl.ds(of, 1)] = jnp.sum(
                jnp.where(diagonal, top[rows], 0.0), axis=0, keepdims=True
            )
            st_send[pl.ds(NZ + of, 1)] = jnp.sum(
                jnp.where(diagonal, o[rows, HEAD:], 0.0), axis=0, keepdims=True
            )

    halves = (pl.ds(0, NA), pl.ds(NA, NZ - NA))
    for d in Z_ORDER:
        send(st_send, st_recv.at[z], "st", "st", dev(dz=d))
    for half in range(2):
        for d in Z_ORDER:
            send(
                o_send.at[(z + d) % NZ, halves[half]], o_recv.at[z, halves[half]],
                f"rs{half}", f"rs{half}", dev(dz=d),
            )
    o_recv[z] = o_send[z]
    st_recv[z] = st_send[...]
    others = pl.ds(1, NZ - 1)
    arrived(turn_all.at[others, 0], "tz")
    for r in YX_ORDER:
        send(turn_all.at[:, yx], turn_all.at[:, yx], "tt", "tt", to_yx(r))
    arrived(st_recv.at[others], "st")
    peaks, totals = st_recv[:, :NZ], st_recv[:, NZ:]
    factor = jnp.exp2(peaks - jnp.max(peaks, axis=0, keepdims=True))
    factor = factor / jnp.sum(factor * totals, axis=0, keepdims=True)
    factors[...] = jnp.concatenate(
        [factor.reshape(NZ * NZ, 128), jnp.zeros((128 - NZ * NZ, 128), F32)], axis=0
    ).T
    factor = factors[pl.ds(pl.multiple_of(16 * z, 16), 16)]
    for at in range(NZ * NZ):
        wide[at] = jnp.broadcast_to(factor[:, at : at + 1], (16, HEAD))

    def attended(half):
        out = []
        for of in (range(NA), range(NA, NZ))[half]:
            num = 0.0
            for j in range(NZ):
                num = num + wide[NZ * j + of] * o_recv[j, of].astype(F32)
            out.append(jnp.concatenate([num[:ROWS], num[ROWS:]], axis=1))
        return jnp.concatenate(out, axis=0).astype(BF16)

    arrived(o_recv.at[others, halves[0]], "rs0")
    part_a[0, 0] = attended(0)
    for i in (1, 2, 3):
        send(part_a.at[0, 0], part_a.at[0, back_y(i)], "a1", f"a1_{back_y(i)}", to_y(i))

    def give(slot, i, steps):
        for step in steps:
            dst = (slot - step) % NZ
            if dst != 4 or (step > 0) == (i < NY // 2):
                got = f"a2_{i}" if dst in (2, 6) else ("a2_side" if dst in (1, 7) else "a2_far")
                send(part_a.at[slot, i], part_a.at[dst, i], "a2", got, dev(dz=step))

    give(0, 0, (1, -1, 2, -2))
    arrived(o_recv.at[others, halves[1]], "rs1")
    part_b[0, 0] = attended(1)
    batch_of = {s: k for k, (lo, hi) in enumerate(Z_BATCHES) for s in range(lo, hi)}
    for d in Z_ORDER:
        slot = ZS.index(NZ - d)
        send(part_b.at[0, 0], part_b.at[slot, 0], "b1", f"b1_{batch_of[slot]}", dev(dz=d))

    def spread(batch):
        lo, hi = Z_BATCHES[batch]
        slots = pl.ds(lo, hi - lo)
        if batch:
            arrived(part_b.at[slots, 0], f"b1_{batch}")
        for i in (1, 2, 3):
            send(part_b.at[slots, 0], part_b.at[slots, back_y(i)], "b2", f"b2_{batch}", to_y(i))

    def spread_arrived(batch):
        lo, hi = Z_BATCHES[batch]
        arrived(part_b.at[pl.ds(lo, hi - lo), pl.ds(1, NY - 1)], f"b2_{batch}")

    def project(part, total, slot, dz, columns):
        at = pl.multiple_of((z + dz) % NZ * 256, 256)
        size = part.shape[1] * part.shape[2]
        new = mm(part[slot].reshape(size, 256), w_all[columns, pl.ds(at, 256)])
        total[columns] = new if dz == 0 else total[columns] + new

    def project_a(slots, columns):
        for slot in slots:
            project(part_a, sum_a, slot, slot, columns)

    def project_b(batches, columns):
        for batch in batches:
            for s in range(*Z_BATCHES[batch]):
                project(part_b, sum_b, s, ZS[s], columns)

    spread(0)
    for i in (1, 2, 3):
        arrived(part_a.at[0, i], f"a1_{i}")
        give(0, i, (1, -1, 2, -2))
        if i == 2:
            spread(1)
    spread(2)
    get_w.wait()
    project_a((0,), 0)
    for i in range(NY):
        arrived(part_a.at[pl.ds(0, 2), i], f"a2_{i}")
        give(6, i, (1, 2))
        give(2, i, (-1, -2))
        if i < 2:
            spread(3 + i)
    arrived(part_a.at[pl.ds(0, 2)], "a2_side")
    project_a((1, 7, 2, 6), 0)
    for batch in range(3):
        spread_arrived(batch)
        project_b((batch,), 0)

    arrived(w_all.at[1], "w")
    project_a((0, 1, 7, 2, 6), 1)
    project_b((0, 1, 2), 1)

    def rows_of(head, size):
        dy = (head + NY - y) % NY
        return pl.ds(pl.multiple_of(size * jnp.where(dy >= 2, 5 - dy, dy), size), size)

    def share(total, sent, got, name, size):
        for columns, d in ((0, 2), (1, 2), (0, 3), (1, 3), (0, 1), (1, 1), (1, 0)):
            slot = NH * columns + d
            back = NH * columns + (NH - d) % NH
            sent[slot] = total[columns, rows_of((h + d) % NH, size)].astype(BF16)
            send(sent.at[slot], got.at[back], name, name, dev(dx=columns, dh=d))

    def finish(total, got, name, first, size):
        arrived(got.at[pl.ds(1, 2 * NH - 1)], name)
        whole = [total[0, rows_of(h, size)], got[NH].astype(F32)]
        for columns in range(2):
            for d in range(1, NH):
                whole[columns] = whole[columns] + got[NH * columns + d].astype(F32)
            for j in range(size // ROWS):
                at = 16 * (first + j) + 8 * ((x + columns) % NX)
                out_ref[pl.ds(pl.multiple_of(at, 8), 8)] = whole[columns][8 * j : 8 * j + 8]
        rows = pl.ds(16 * first, 2 * size)
        outs.append(put(out_ref.at[rows], out_hbm.at[rows], 2 + (first > 0)))

    for batch in (3, 4):
        spread_arrived(batch)
    project_b((3, 4), 0)
    project_b((3, 4), 1)
    share(sum_b, hb_send, hb_recv, "hb", RB)
    arrived(part_a.at[pl.ds(3, 3)], "a2_far")
    project_a((3, 5, 4), 0)
    project_a((3, 5, 4), 1)
    share(sum_a, ha_send, ha_recv, "ha", RA)

    arrived(turn_all.at[:, pl.ds(1, NYX - 1)], "tt")
    col = iota((128, 1024), 1)
    of_piece = 32 * (col // 32 % 4) + 4 * (col // 128) + 2 * (col // 16 % 2) + col // 4 % 2
    slot_of = mm(
        jnp.broadcast_to(slots_ref[...], (16, 128)).astype(BF16),
        (iota((128, 1024), 0) == of_piece).astype(BF16),
    ).astype(jnp.int32)
    row, col = iota((16, 1024), 0), iota((16, 1024), 1)
    chosen = (slot_of == 4 * c + row // 4) & (col % 4 == row % 4)
    every = turn_all[...].reshape(1024, HEAD)
    kind = col // 8 % 2
    ak_ref[...] = mm((chosen & (kind == 0)).astype(BF16), every).astype(BF16)
    av_ref[...] = mm((chosen & (kind == 1)).astype(BF16), every).astype(BF16)
    outs = [put(ak_ref, ak_hbm, 0), put(av_ref, av_hbm, 1)]

    finish(sum_b, hb_recv, "hb", NA, RB)
    left(q_all.at[others], "q")
    left(k_all.at[others], "k")
    left(v_all.at[others], "v")
    left(turn_yx.at[others], "t")
    left(turn_yx.at[others], "tz")
    left(turn_all.at[others], "tt")
    left(st_recv.at[others], "st")
    for half in range(2):
        left(o_recv.at[others, halves[half]], f"rs{half}")
    left(part_a.at[0, pl.ds(1, NY - 1)], "a1")
    left(part_b.at[others, 0], "b1")
    left(part_a.at[others], "a2")
    left(part_b.at[:, pl.ds(1, NY - 1)], "b2")
    left(w_all.at[1], "w")
    left(hb_send.at[others], "hb")
    finish(sum_a, ha_recv, "ha", 0, RA)
    left(ha_send.at[others], "ha")
    for cp in outs:
        cp.wait()


def write_out(a_in, b_in, c_in, a_out, b_out, c_out, a_mid, b_mid, c_mid, sems):
    ins = [(a_in, a_mid), (b_in, b_mid), (c_in, c_mid)]
    outs = [(a_mid, a_out), (b_mid, b_out), (c_mid, c_out)]
    ins = [pltpu.make_async_copy(*pair, sems.at[0, i]) for i, pair in enumerate(ins)]
    outs = [pltpu.make_async_copy(*pair, sems.at[1, i]) for i, pair in enumerate(outs)]
    for cp in ins:
        cp.start()
    for i in (1, 2, 0):
        ins[i].wait()
        outs[i].start()
    for cp in outs:
        cp.wait()


def on_device(
    queries, cache_keys, stored_cache_values, turn_keys, turn_values,
    block_mask, doc_ids, slot_ids, out_weight,
):
    anywhere = pl.BlockSpec(memory_space=pl.ANY)
    results = pl.pallas_call(
        kernel,
        out_shape=(
            jax.ShapeDtypeStruct((128, 256), F32),
            jax.ShapeDtypeStruct((16, HEAD), BF16),
            jax.ShapeDtypeStruct((16, HEAD), BF16),
        ),
        in_specs=[anywhere] * 9,
        out_specs=(anywhere,) * 3,
        scratch_shapes=[
            pltpu.VMEM((128, HEAD), BF16),
            pltpu.VMEM((NZ, 128, HEAD), BF16),
            pltpu.VMEM((NYX, KEYS, HEAD), BF16),
            pltpu.VMEM((NYX, KEYS, HEAD), BF16),
            pltpu.VMEM((4, 2 * KEYS, 2 * HEAD), BF16),
            pltpu.VMEM((NX, 2048, 256), BF16),
            pltpu.VMEM((NYX, 16, HEAD), BF16),
            pltpu.VMEM((NZ, NYX, 16, HEAD), BF16),
            pltpu.VMEM((ROWS, HEAD), BF16),
            pltpu.VMEM((ROWS, HEAD), BF16),
            pltpu.VMEM((NY, 128), jnp.int32),
            pltpu.VMEM((1, 128), jnp.int32),
            pltpu.SMEM((NY, 128), jnp.int32),
            pltpu.VMEM((4, 256, 128), F32),
            pltpu.VMEM((4, 256, 256), F32),
            pltpu.VMEM((NZ, NZ, 16, HEAD), BF16),
            pltpu.VMEM((2 * NZ, 128), F32),
            pltpu.VMEM((NZ, NZ, 16, HEAD), BF16),
            pltpu.VMEM((NZ, 2 * NZ, 128), F32),
            pltpu.VMEM((128, 128), F32),
            pltpu.VMEM((NZ * NZ, 16, HEAD), F32),
            pltpu.VMEM((NZ, 128, 128), F32),
            pltpu.VMEM((NZ, NY, RA, 256), BF16),
            pltpu.VMEM((NZ, NY, RB, 256), BF16),
            pltpu.VMEM((NX, NY * RA, 256), F32),
            pltpu.VMEM((NX, NY * RB, 256), F32),
            pltpu.VMEM((2 * NH, RA, 256), BF16),
            pltpu.VMEM((2 * NH, RA, 256), BF16),
            pltpu.VMEM((2 * NH, RB, 256), BF16),
            pltpu.VMEM((2 * NH, RB, 256), BF16),
            pltpu.VMEM((128, 256), F32),
            pltpu.VMEM((16, HEAD), BF16),
            pltpu.VMEM((16, HEAD), BF16),
            pltpu.SemaphoreType.DMA((9,)),
            pltpu.SemaphoreType.DMA((4,)),
            pltpu.SemaphoreType.DMA((len(SENT),)),
            pltpu.SemaphoreType.DMA((len(GOT),)),
        ],
        compiler_params=pltpu.CompilerParams(
            collective_id=0, has_side_effects=True, vmem_limit_bytes=60 * 1024 * 1024
        ),
        name="turn_attention",
    )(
        queries.reshape(128, HEAD),
        cache_keys.reshape(KEYS, HEAD),
        stored_cache_values.reshape(KEYS, HEAD),
        out_weight,
        turn_keys.reshape(ROWS, HEAD),
        turn_values.reshape(ROWS, HEAD),
        doc_ids.reshape(NY, 128),
        slot_ids.reshape(1, 128),
        block_mask,
    )
    layer_out, append_keys, append_values = pl.pallas_call(
        write_out,
        out_shape=tuple(jax.ShapeDtypeStruct(r.shape, r.dtype) for r in results),
        in_specs=[anywhere] * 3,
        out_specs=(anywhere,) * 3,
        scratch_shapes=[pltpu.VMEM(r.shape, r.dtype) for r in results]
        + [pltpu.SemaphoreType.DMA((2, 3))],
        compiler_params=pltpu.CompilerParams(vmem_limit_bytes=60 * 1024 * 1024),
        name="write_out",
    )(*results)
    return (
        layer_out,
        append_keys.reshape(16, 1, HEAD),
        append_values.reshape(16, 1, HEAD),
    )


def solution(mesh):
    placed = (
        P("ctx", "head", None),
        P("ctx", "head", None),
        P("ctx", "head", None),
        P("ctx", "head", None),
        P("ctx", "head", None),
        P(),
        P(),
        P(),
        P("head", "ctx"),
    )
    return jax.shard_map(
        on_device,
        mesh=mesh,
        in_specs=placed,
        out_specs=(P("head", "ctx"), P("ctx", "head", None), P("ctx", "head", None)),
        check_vma=False,
    )
```

```python
import math

import jax
import jax.numpy as jnp
from jax import lax
from jax.experimental import pallas as pl
from jax.experimental.pallas import tpu as pltpu
from jax.sharding import PartitionSpec as P

MESH = pl.DeviceIdType.MESH
F32 = jnp.float32
BF16 = jnp.bfloat16

NY, NZ, NX = 4, 8, 2
NYX = NY * NX
NH = 4
HEAD = 128
KEYS = 256
GROUP = 16
ROWS = 8
NEG = -1e30
FLOOR = -1e29
SCALE = math.log2(math.e) / math.sqrt(HEAD)

YX = [(0, 0), (0, 1), (1, 0), (1, 1), (3, 0), (3, 1), (2, 0), (2, 1)]
YX_ORDER = [1, 2, 4, 3, 5, 6, 7]
YS = [0, 1, 3, 2]
ZS = [0, 1, 7, 2, 6, 3, 5, 4]
Z_ORDER = [1, 7, 2, 6, 3, 5, 4]
Z_BATCHES = [(0, 1), (1, 3), (3, 5), (5, 7), (7, 8)]
NA = 4
RA, RB = NA * ROWS, (NZ - NA) * ROWS
DIRECT = True
SENT = [
    "q", "k", "v", "t", "tz", "tt", "st", "rs", "a1", "b1", "a2", "b2", "ha", "hb", "w",
]
GOT = [
    "q0", "q1", "q2", "q3", "v1", "k1", "k2", "k4", "k6", "g1", "g2", "g3", "t", "tz", "tt", "st",
    "rs", "a1_1", "a1_2", "a1_3", "b1_1", "b1_2", "b1_3", "b1_4", "a2_0", "a2_1", "a2_2",
    "a2_3", "a2_side", "a2_far", "b2_0", "b2_1", "b2_2", "b2_3", "b2_4", "ha", "hb", "w",
]
KEY_GROUPS = [(0, 1), (2, 4), (6, 3), (5, 7)]
BLOCKS = [
    (0, 0), (0, 1), (1, 0), (1, 1), (0, 2), (1, 2), (2, 0), (2, 1), (2, 2), (0, 3), (1, 3), (2, 3),
    (3, 0), (3, 1), (3, 2), (3, 3),
]


def nt(a, b):
    return lax.dot_general(a, b, (((1,), (1,)), ((), ())), preferred_element_type=F32)


def mm(a, b):
    return jnp.dot(a, b, preferred_element_type=F32)


def iota(shape, dim):
    return lax.broadcasted_iota(jnp.int32, shape, dim)


def around(i, step, size):
    return lax.rem(i + step % size, size) if step % size else i


def back_yx(r):
    dy, dx = YX[r]
    return YX.index(((NY - dy) % NY, dx))


def kernel(
    q_in, ck_in, cv_in, w_in, tk_in, tv_in, doc_in, slot_in, mask_in,
    out_hbm, ak_hbm, av_hbm,
    q_raw, q_all, k_all, v_all, v_wide, w_all, turn_yx, turn_all, tk, tv, docs_ref, slots_ref, mask_ref,
    peak, acc, o_send, st_send, o_recv, st_recv, factors, wide, sights, part_a, part_b, sum_a, sum_b,
    ha_send, ha_recv, hb_send, hb_recv, out_ref, ak_ref, av_ref,
    sem_in, sem_out, sem_sent, sem_got,
):
    c = lax.axis_index("ctx")
    h = lax.axis_index("head")
    y, z, x = lax.div(c, NZ * NX), lax.rem(lax.div(c, NX), NZ), lax.rem(c, NX)
    yx = y * NX + x

    def dev(dy=0, dz=0, dx=0, dh=0):
        ty, tz, tx = around(y, dy, NY), around(z, dz, NZ), around(x, dx, NX)
        return ((ty * NZ + tz) * NX + tx, around(h, dh, NH))

    def to_y(i):
        return dev(dy=YS[i])

    def back_y(i):
        return YS.index((NY - YS[i]) % NY)

    def to_yx(r):
        return dev(dy=YX[r][0], dx=YX[r][1])

    def send(src, dst, sent, got, device):
        pltpu.make_async_remote_copy(
            src_ref=src, dst_ref=dst, send_sem=sem_sent.at[SENT.index(sent)],
            recv_sem=sem_got.at[GOT.index(got)], device_id=device, device_id_type=MESH,
        ).start()

    def arrived(ref, got):
        pltpu.make_async_copy(ref, ref, sem_got.at[GOT.index(got)]).wait()

    def left(ref, sent):
        pltpu.make_async_copy(ref, ref, sem_sent.at[SENT.index(sent)]).wait()

    def put(src, dst, i):
        copy = pltpu.make_async_copy(src, dst, sem_out.at[i])
        copy.start()
        return copy

    def fetch(src, dst, i):
        copy = pltpu.make_async_copy(src, dst, sem_in.at[i])
        copy.start()
        return copy

    barrier = pltpu.get_barrier_semaphore()
    peers = [to_yx(r) for r in YX_ORDER] + [dev(dz=d) for d in Z_ORDER]
    peers += [dev(dx=dx, dh=d) for dx in range(NX) for d in range(1, NH)]
    for p in peers:
        pl.semaphore_signal(barrier, inc=1, device_id=p, device_id_type=MESH)

    get_q = fetch(q_in, q_raw, 0)
    get_small = [
        fetch(tk_in, tk, 1), fetch(tv_in, tv, 2), fetch(doc_in, docs_ref, 3),
        fetch(slot_in, slots_ref, 4), fetch(mask_in, mask_ref, 5),
    ]
    get_kv = [fetch(ck_in, k_all.at[0], 6), fetch(cv_in, v_all.at[0], 7)]
    get_w = fetch(w_in, w_all.at[0], 8)

    pl.semaphore_wait(barrier, len(peers))

    def give_k(src, slot, device):
        got = f"k{slot}" if slot in (1, 2, 4, 6) else ("g2" if slot == 3 else "g3")
        send(src, k_all.at[slot], "k", got, device)

    def give_v(src, slot, device):
        got = {1: "v1", 2: "g1", 4: "g1", 3: "g2", 6: "g2"}.get(slot, "g3")
        send(src, v_all.at[slot], "v", got, device)

    give_v(cv_in, 1, to_yx(1))
    for r in (2, 4, 6):
        give_k(ck_in, back_yx(r), to_yx(r))
    give_k(ck_in, 1, to_yx(1))
    for r in (2, 4, 6):
        give_v(cv_in, back_yx(r), to_yx(r))

    get_q.wait()
    i0, i1 = iota((128, 128), 0), iota((128, 128), 1)
    order = (i1 == (i0 % ROWS) * GROUP + i0 // ROWS).astype(BF16)
    q_all[0] = mm(order, q_raw[...]).astype(BF16)
    for d in Z_ORDER:
        slot = ZS.index(NZ - d)
        send(q_all.at[0], q_all.at[slot], "q", f"q{slot // 2}", dev(dz=d))
    for cp in get_small:
        cp.wait()
    mine = jnp.concatenate([tk[...].astype(F32), tv[...].astype(F32)], axis=0).astype(BF16)
    turn_yx[yx] = mine
    turn_all[z, yx] = mine
    for r in YX_ORDER:
        send(turn_yx.at[yx], turn_yx.at[yx], "t", "t", to_yx(r))
    for d in Z_ORDER:
        send(turn_yx.at[yx], turn_all.at[z, yx], "tz", "tz", dev(dz=d))

    docs = docs_ref[...]
    key_token = 16 * z + 8 * (i1 // 16 % 2) + i1 % 8
    by_y = mm(
        jnp.concatenate([docs.astype(F32), jnp.zeros((12, 128), F32)], axis=0).astype(BF16),
        (i0 == key_token).astype(BF16),
    )
    key_doc = jnp.sum(
        jnp.where(iota((16, 128), 0) == iota((16, 128), 1) // 32, by_y, 0.0), axis=0, keepdims=True
    )
    doc_mine = jnp.sum(
        jnp.where(iota((NY, 128), 0) == y, docs, 0), axis=0, keepdims=True
    ).astype(F32)
    right_key = (i1 // 8 % 2 == 0)

    def sight(slot):
        query_token = 16 * around(z, ZS[slot], NZ) + 8 * x + i0 % 8
        query_doc = jnp.sum(jnp.where(i1 == query_token, doc_mine, 0.0), axis=1, keepdims=True)
        see = (
            (128 * (i1 // 32) + key_token <= 128 * y + query_token)
            & (key_doc == query_doc)
            & right_key
        )
        return jnp.where(see, 0.0, NEG)

    diagonal = i0 == i1

    arrived(v_all.at[1], "v1")
    for r in (2, 4, 6):
        give_v(v_all.at[1], back_yx(r + 1), to_yx(r))
    for slot in range(NZ):
        sights[slot] = sight(slot)
    for r in (2, 4, 6):
        arrived(k_all.at[r], f"k{r}")
        give_k(k_all.at[r], r + 1, to_yx(1))
    send(w_in, w_all.at[1], "w", "w", dev(dx=1))

    biases = {}
    for g, i in BLOCKS:
        last = g == 3
        if i == 0:
            if g == 0:
                for cp in get_kv:
                    cp.wait()
                arrived(k_all.at[1], "k1")
            else:
                arrived(k_all.at[pl.ds(0, g + 1)], f"g{g}")
            for j, r in enumerate(KEY_GROUPS[g]):
                v_wide[g, KEYS * j : KEYS * (j + 1), :HEAD] = v_all[r]
            v_wide[g, :, HEAD:] = jnp.ones((2 * KEYS, HEAD), BF16)
            biases[g] = []
            for r in KEY_GROUPS[g]:
                source = (around(y, YX[r][0], NY) * NZ + z) * NX + around(x, YX[r][1], NX)
                for b in range(2):
                    biases[g].append(jnp.where(mask_ref[y, 2 * source + b] == 1, 0.0, NEG))
            if last:
                arrived(turn_yx.at[pl.ds(1, NYX - 1)], "t")
                fresh = turn_yx[...].reshape(128, HEAD)
                fresh_v = mm((i1 == i0 + 8).astype(BF16), fresh).astype(BF16)
                fresh_v = jnp.concatenate([fresh_v, jnp.ones((128, HEAD), BF16)], axis=1)
        if g == 0:
            arrived(q_all.at[pl.ds(2 * i, 2)] if i else q_all.at[1], f"q{i}")
        q = q_all[2 * i : 2 * i + 2].reshape(256, HEAD)
        parts = []
        for j, r in enumerate(KEY_GROUPS[g]):
            s = nt(q, k_all[r])
            parts += [
                s[:, :128] * SCALE + biases[g][2 * j], s[:, 128:] * SCALE + biases[g][2 * j + 1]
            ]
        values = v_wide[g]
        if last:
            parts.append(nt(q, fresh) * SCALE + sights[2 * i : 2 * i + 2].reshape(256, 128))
            values = jnp.concatenate([values, fresh_v], axis=0)
        top = parts[0]
        for p in parts[1:]:
            top = jnp.maximum(top, p)
        top = jnp.broadcast_to(jnp.max(top, axis=1, keepdims=True), (256, 128))
        old = FLOOR if g == 0 else peak[i]
        top = jnp.maximum(top, old)
        p = jnp.concatenate([jnp.exp2(p - top).astype(BF16) for p in parts], axis=1)
        o = mm(p, values)
        if g > 0:
            keep = jnp.exp2(old - top)
            o = o + acc[i] * jnp.concatenate([keep, keep], axis=1)
        if not last:
            acc[i] = o
            peak[i] = top
            continue
        for j in range(2):
            rows = slice(128 * j, 128 * (j + 1))
            of = around(z, ZS[2 * i + j], NZ)
            o_send[:, of] = o[rows, :HEAD].astype(BF16).reshape(NZ, 16, HEAD)
            st_send[pl.ds(of, 1)] = jnp.sum(
                jnp.where(diagonal, top[rows], 0.0), axis=0, keepdims=True
            )
            st_send[pl.ds(NZ + of, 1)] = jnp.sum(
                jnp.where(diagonal, o[rows, HEAD:], 0.0), axis=0, keepdims=True
            )

    for d in Z_ORDER:
        send(st_send, st_recv.at[z], "st", "st", dev(dz=d))
    for d in (4, 3, 5, 2, 6, 1, 7):
        send(o_send.at[around(z, d, NZ)], o_recv.at[z], "rs", "rs", dev(dz=d))
    o_recv[z] = o_send[z]
    st_recv[z] = st_send[...]
    others = pl.ds(1, NZ - 1)
    arrived(turn_all.at[others, 0], "tz")
    for r in YX_ORDER:
        send(turn_all.at[:, yx], turn_all.at[:, yx], "tt", "tt", to_yx(r))
    arrived(st_recv.at[others], "st")
    peaks, totals = st_recv[:, :NZ], st_recv[:, NZ:]
    factor = jnp.exp2(peaks - jnp.max(peaks, axis=0, keepdims=True))
    factor = factor / jnp.sum(factor * totals, axis=0, keepdims=True)
    factors[...] = jnp.concatenate(
        [factor.reshape(NZ * NZ, 128), jnp.zeros((128 - NZ * NZ, 128), F32)], axis=0
    ).T
    factor = factors[pl.ds(pl.multiple_of(16 * z, 16), 16)]
    for at in range(NZ * NZ):
        wide[at] = jnp.broadcast_to(factor[:, at : at + 1], (16, HEAD))

    def attended(half):
        out = []
        for of in (range(NA), range(NA, NZ))[half]:
            num = 0.0
            for j in range(NZ):
                num = num + wide[NZ * j + of] * o_recv[j, of].astype(F32)
            out.append(jnp.concatenate([num[:ROWS], num[ROWS:]], axis=1))
        return jnp.concatenate(out, axis=0).astype(BF16)

    arrived(o_recv.at[others], "rs")
    part_a[0, 0] = attended(0)
    for i in (1, 2, 3):
        send(part_a.at[0, 0], part_a.at[0, back_y(i)], "a1", f"a1_{back_y(i)}", to_y(i))

    def give(slot, i, steps):
        for step in steps:
            dst = (slot - step) % NZ
            if dst != 4 or (step > 0) == (i < NY // 2):
                got = f"a2_{i}" if dst in (2, 6) else ("a2_side" if dst in (1, 7) else "a2_far")
                send(part_a.at[slot, i], part_a.at[dst, i], "a2", got, dev(dz=step))

    give(0, 0, (1, -1, 2, -2))
    part_b[0, 0] = attended(1)
    batch_of = {s: k for k, (lo, hi) in enumerate(Z_BATCHES) for s in range(lo, hi)}
    for d in Z_ORDER:
        slot = ZS.index(NZ - d)
        send(part_b.at[0, 0], part_b.at[slot, 0], "b1", f"b1_{batch_of[slot]}", dev(dz=d))

    def spread(batch):
        lo, hi = Z_BATCHES[batch]
        slots = pl.ds(lo, hi - lo)
        if batch:
            arrived(part_b.at[slots, 0], f"b1_{batch}")
        for i in (1, 2, 3):
            send(part_b.at[slots, 0], part_b.at[slots, back_y(i)], "b2", f"b2_{batch}", to_y(i))

    def spread_arrived(batch):
        lo, hi = Z_BATCHES[batch]
        arrived(part_b.at[pl.ds(lo, hi - lo), pl.ds(1, NY - 1)], f"b2_{batch}")

    def project(part, total, slot, dz, columns):
        at = pl.multiple_of(around(z, dz, NZ) * 256, 256)
        size = part.shape[1] * part.shape[2]
        new = mm(part[slot].reshape(size, 256), w_all[columns, pl.ds(at, 256)])
        total[columns] = new if dz == 0 else total[columns] + new

    def project_a(slots, columns):
        for slot in slots:
            project(part_a, sum_a, slot, slot, columns)

    def project_b(batches, columns):
        for batch in batches:
            for s in range(*Z_BATCHES[batch]):
                project(part_b, sum_b, s, ZS[s], columns)

    spread(0)
    for i in (1, 2, 3):
        arrived(part_a.at[0, i], f"a1_{i}")
        give(0, i, (1, -1, 2, -2))
        if i == 2:
            spread(1)
    spread(2)
    get_w.wait()
    project_a((0,), 0)
    for i in range(NY):
        arrived(part_a.at[pl.ds(0, 2), i], f"a2_{i}")
        give(6, i, (1, 2))
        give(2, i, (-1, -2))
        if i < 2:
            spread(3 + i)
    arrived(part_a.at[pl.ds(0, 2)], "a2_side")
    project_a((1, 7, 2, 6), 0)
    for batch in range(3):
        spread_arrived(batch)
        project_b((batch,), 0)

    arrived(w_all.at[1], "w")
    project_a((0, 1, 7, 2, 6), 1)
    project_b((0, 1, 2), 1)

    def rows_of(head, size):
        dy = lax.rem(head + NY - y, NY)
        return pl.ds(pl.multiple_of(size * jnp.where(dy >= 2, 5 - dy, dy), size), size)

    def share(total, sent, got, name, size):
        for columns, d in ((0, 2), (1, 2), (0, 3), (1, 3), (0, 1), (1, 1), (1, 0)):
            slot = NH * columns + d
            back = NH * columns + (NH - d) % NH
            sent[slot] = total[columns, rows_of(around(h, d, NH), size)].astype(BF16)
            send(sent.at[slot], got.at[back], name, name, dev(dx=columns, dh=d))

    def finish(total, got, name, first, size):
        arrived(got.at[pl.ds(1, 2 * NH - 1)], name)
        whole = [total[0, rows_of(h, size)], got[NH].astype(F32)]
        for columns in range(2):
            for d in range(1, NH):
                whole[columns] = whole[columns] + got[NH * columns + d].astype(F32)
            for j in range(size // ROWS):
                at = 16 * (first + j) + 8 * around(x, columns, NX)
                out_ref[pl.ds(pl.multiple_of(at, 8), 8)] = whole[columns][8 * j : 8 * j + 8]
        rows = pl.ds(16 * first, 2 * size)
        outs.append(put(out_ref.at[rows], out_hbm.at[rows], 2 + (first > 0)))

    for batch in (3, 4):
        spread_arrived(batch)
    project_b((3, 4), 0)
    project_b((3, 4), 1)
    share(sum_b, hb_send, hb_recv, "hb", RB)
    arrived(part_a.at[pl.ds(3, 3)], "a2_far")
    project_a((3, 5, 4), 0)
    project_a((3, 5, 4), 1)
    share(sum_a, ha_send, ha_recv, "ha", RA)

    arrived(turn_all.at[:, pl.ds(1, NYX - 1)], "tt")
    col = iota((128, 1024), 1)
    of_piece = 32 * (col // 32 % 4) + 4 * (col // 128) + 2 * (col // 16 % 2) + col // 4 % 2
    slot_of = mm(
        jnp.broadcast_to(slots_ref[...], (16, 128)).astype(BF16),
        (iota((128, 1024), 0) == of_piece).astype(BF16),
    ).astype(jnp.int32)
    row, col = iota((16, 1024), 0), iota((16, 1024), 1)
    chosen = (slot_of == 4 * c + row // 4) & (col % 4 == row % 4)
    every = turn_all[...].reshape(1024, HEAD)
    kind = col // 8 % 2
    ak_ref[...] = mm((chosen & (kind == 0)).astype(BF16), every).astype(BF16)
    av_ref[...] = mm((chosen & (kind == 1)).astype(BF16), every).astype(BF16)
    outs = [put(ak_ref, ak_hbm, 0), put(av_ref, av_hbm, 1)]

    finish(sum_b, hb_recv, "hb", NA, RB)
    left(q_all.at[others], "q")
    left(k_all.at[others], "k")
    left(v_all.at[others], "v")
    left(turn_yx.at[others], "t")
    left(turn_yx.at[others], "tz")
    left(turn_all.at[others], "tt")
    left(st_recv.at[others], "st")
    left(o_recv.at[others], "rs")
    left(part_a.at[0, pl.ds(1, NY - 1)], "a1")
    left(part_b.at[others, 0], "b1")
    left(part_a.at[others], "a2")
    left(part_b.at[:, pl.ds(1, NY - 1)], "b2")
    left(w_all.at[1], "w")
    left(hb_send.at[others], "hb")
    finish(sum_a, ha_recv, "ha", 0, RA)
    left(ha_send.at[others], "ha")
    for cp in outs:
        cp.wait()


def write_out(a_in, b_in, c_in, a_out, b_out, c_out, a_mid, b_mid, c_mid, sems):
    ins = [(a_in, a_mid), (b_in, b_mid), (c_in, c_mid)]
    outs = [(a_mid, a_out), (b_mid, b_out), (c_mid, c_out)]
    ins = [pltpu.make_async_copy(*pair, sems.at[0, i]) for i, pair in enumerate(ins)]
    outs = [pltpu.make_async_copy(*pair, sems.at[1, i]) for i, pair in enumerate(outs)]
    for cp in ins:
        cp.start()
    for i in (1, 2, 0):
        ins[i].wait()
        outs[i].start()
    for cp in outs:
        cp.wait()


def on_device(
    queries, cache_keys, stored_cache_values, turn_keys, turn_values,
    block_mask, doc_ids, slot_ids, out_weight,
):
    anywhere = pl.BlockSpec(memory_space=pl.ANY)
    results = pl.pallas_call(
        kernel,
        out_shape=(
            jax.ShapeDtypeStruct((128, 256), F32),
            jax.ShapeDtypeStruct((16, HEAD), BF16),
            jax.ShapeDtypeStruct((16, HEAD), BF16),
        ),
        in_specs=[anywhere] * 9,
        out_specs=(anywhere,) * 3,
        scratch_shapes=[
            pltpu.VMEM((128, HEAD), BF16),
            pltpu.VMEM((NZ, 128, HEAD), BF16),
            pltpu.VMEM((NYX, KEYS, HEAD), BF16),
            pltpu.VMEM((NYX, KEYS, HEAD), BF16),
            pltpu.VMEM((4, 2 * KEYS, 2 * HEAD), BF16),
            pltpu.VMEM((NX, 2048, 256), BF16),
            pltpu.VMEM((NYX, 16, HEAD), BF16),
            pltpu.VMEM((NZ, NYX, 16, HEAD), BF16),
            pltpu.VMEM((ROWS, HEAD), BF16),
            pltpu.VMEM((ROWS, HEAD), BF16),
            pltpu.VMEM((NY, 128), jnp.int32),
            pltpu.VMEM((1, 128), jnp.int32),
            pltpu.SMEM((NY, 128), jnp.int32),
            pltpu.VMEM((4, 256, 128), F32),
            pltpu.VMEM((4, 256, 256), F32),
            pltpu.VMEM((NZ, NZ, 16, HEAD), BF16),
            pltpu.VMEM((2 * NZ, 128), F32),
            pltpu.VMEM((NZ, NZ, 16, HEAD), BF16),
            pltpu.VMEM((NZ, 2 * NZ, 128), F32),
            pltpu.VMEM((128, 128), F32),
            pltpu.VMEM((NZ * NZ, 16, HEAD), F32),
            pltpu.VMEM((NZ, 128, 128), F32),
            pltpu.VMEM((NZ, NY, RA, 256), BF16),
            pltpu.VMEM((NZ, NY, RB, 256), BF16),
            pltpu.VMEM((NX, NY * RA, 256), F32),
            pltpu.VMEM((NX, NY * RB, 256), F32),
            pltpu.VMEM((2 * NH, RA, 256), BF16),
            pltpu.VMEM((2 * NH, RA, 256), BF16),
            pltpu.VMEM((2 * NH, RB, 256), BF16),
            pltpu.VMEM((2 * NH, RB, 256), BF16),
            pltpu.VMEM((128, 256), F32),
            pltpu.VMEM((16, HEAD), BF16),
            pltpu.VMEM((16, HEAD), BF16),
            pltpu.SemaphoreType.DMA((9,)),
            pltpu.SemaphoreType.DMA((4,)),
            pltpu.SemaphoreType.DMA((len(SENT),)),
            pltpu.SemaphoreType.DMA((len(GOT),)),
        ],
        compiler_params=pltpu.CompilerParams(
            collective_id=0, has_side_effects=True, vmem_limit_bytes=60 * 1024 * 1024
        ),
        name="turn_attention",
    )(
        queries.reshape(128, HEAD),
        cache_keys.reshape(KEYS, HEAD),
        stored_cache_values.reshape(KEYS, HEAD),
        out_weight,
        turn_keys.reshape(ROWS, HEAD),
        turn_values.reshape(ROWS, HEAD),
        doc_ids.reshape(NY, 128),
        slot_ids.reshape(1, 128),
        block_mask,
    )
    layer_out, append_keys, append_values = pl.pallas_call(
        write_out,
        out_shape=tuple(jax.ShapeDtypeStruct(r.shape, r.dtype) for r in results),
        in_specs=[anywhere] * 3,
        out_specs=(anywhere,) * 3,
        scratch_shapes=[pltpu.VMEM(r.shape, r.dtype) for r in results]
        + [pltpu.SemaphoreType.DMA((2, 3))],
        compiler_params=pltpu.CompilerParams(vmem_limit_bytes=60 * 1024 * 1024),
        name="write_out",
    )(*results)
    return (
        layer_out,
        append_keys.reshape(16, 1, HEAD),
        append_values.reshape(16, 1, HEAD),
    )


def solution(mesh):
    placed = (
        P("ctx", "head", None),
        P("ctx", "head", None),
        P("ctx", "head", None),
        P("ctx", "head", None),
        P("ctx", "head", None),
        P(),
        P(),
        P(),
        P("head", "ctx"),
    )
    return jax.shard_map(
        on_device,
        mesh=mesh,
        in_specs=placed,
        out_specs=(P("head", "ctx"), P("ctx", "head", None), P("ctx", "head", None)),
        check_vma=False,
    )
```

```python
import math

import jax
import jax.numpy as jnp
from jax import lax
from jax.experimental import pallas as pl
from jax.experimental.pallas import tpu as pltpu
from jax.sharding import PartitionSpec as P

MESH = pl.DeviceIdType.MESH
F32 = jnp.float32
BF16 = jnp.bfloat16

NY, NZ, NX = 4, 8, 2
NYX = NY * NX
NH = 4
HEAD = 128
KEYS = 256
GROUP = 16
ROWS = 8
NEG = -1e30
FLOOR = -1e29
SCALE = math.log2(math.e) / math.sqrt(HEAD)

YX = [(0, 0), (0, 1), (1, 0), (1, 1), (3, 0), (3, 1), (2, 0), (2, 1)]
YX_ORDER = [1, 2, 4, 3, 5, 6, 7]
YS = [0, 1, 3, 2]
ZS = [0, 1, 7, 2, 6, 3, 5, 4]
Z_ORDER = [1, 7, 2, 6, 3, 5, 4]
Z_BATCHES = [(0, 1), (1, 3), (3, 5), (5, 7), (7, 8)]
NA = 4
RA, RB = NA * ROWS, (NZ - NA) * ROWS
DIRECT = True
SENT = [
    "q", "k", "v", "t", "tz", "tt", "st", "rs", "a1", "b1", "a2", "b2", "ha", "hb", "w",
]
GOT = [
    "q0", "q1", "q2", "q3", "v1", "k1", "k2", "k4", "k6", "g1", "g2", "g3", "t", "tz", "tt", "st",
    "rs", "a1_1", "a1_2", "a1_3", "b1_1", "b1_2", "b1_3", "b1_4", "a2_0", "a2_1", "a2_2",
    "a2_3", "a2_side", "a2_far", "b2_0", "b2_1", "b2_2", "b2_3", "b2_4", "ha", "hb", "w",
]
KEY_GROUPS = [(0, 1), (2, 4), (6, 3), (5, 7)]
BLOCKS = [
    (0, 0), (0, 1), (1, 0), (1, 1), (0, 2), (1, 2), (2, 0), (2, 1), (2, 2), (0, 3), (1, 3), (2, 3),
    (3, 0), (3, 1), (3, 2), (3, 3),
]


def nt(a, b):
    return lax.dot_general(a, b, (((1,), (1,)), ((), ())), preferred_element_type=F32)


def mm(a, b):
    return jnp.dot(a, b, preferred_element_type=F32)


def iota(shape, dim):
    return lax.broadcasted_iota(jnp.int32, shape, dim)


def around(i, step, size):
    return lax.rem(i + step % size, size) if step % size else i


def back_yx(r):
    dy, dx = YX[r]
    return YX.index(((NY - dy) % NY, dx))


def kernel(
    q_in, ck_in, cv_in, w_in, tk_in, tv_in, doc_in, slot_in, mask_in,
    out_hbm, ak_hbm, av_hbm,
    q_raw, q_all, k_all, v_all, v_wide, w_all, turn_yx, turn_all, tk, tv, docs_ref, slots_ref, mask_ref,
    peak, acc, o_send, st_send, o_recv, st_recv, factors, wide, sights, part_a, part_b, sum_a, sum_b,
    ha_send, ha_recv, hb_send, hb_recv, out_ref, ak_ref, av_ref,
    sem_in, sem_out, sem_sent, sem_got,
):
    c = lax.axis_index("ctx")
    h = lax.axis_index("head")
    y, z, x = lax.div(c, NZ * NX), lax.rem(lax.div(c, NX), NZ), lax.rem(c, NX)
    yx = y * NX + x

    def dev(dy=0, dz=0, dx=0, dh=0):
        ty, tz, tx = around(y, dy, NY), around(z, dz, NZ), around(x, dx, NX)
        return ((ty * NZ + tz) * NX + tx, around(h, dh, NH))

    def to_y(i):
        return dev(dy=YS[i])

    def back_y(i):
        return YS.index((NY - YS[i]) % NY)

    def to_yx(r):
        return dev(dy=YX[r][0], dx=YX[r][1])

    def send(src, dst, sent, got, device):
        pltpu.make_async_remote_copy(
            src_ref=src, dst_ref=dst, send_sem=sem_sent.at[SENT.index(sent)],
            recv_sem=sem_got.at[GOT.index(got)], device_id=device, device_id_type=MESH,
        ).start()

    def arrived(ref, got):
        pltpu.make_async_copy(ref, ref, sem_got.at[GOT.index(got)]).wait()

    def left(ref, sent):
        pltpu.make_async_copy(ref, ref, sem_sent.at[SENT.index(sent)]).wait()

    def put(src, dst, i):
        copy = pltpu.make_async_copy(src, dst, sem_out.at[i])
        copy.start()
        return copy

    def fetch(src, dst, i):
        copy = pltpu.make_async_copy(src, dst, sem_in.at[i])
        copy.start()
        return copy

    barrier = pltpu.get_barrier_semaphore()
    peers = [to_yx(r) for r in YX_ORDER] + [dev(dz=d) for d in Z_ORDER]
    peers += [dev(dx=dx, dh=d) for dx in range(NX) for d in range(1, NH)]
    for p in peers:
        pl.semaphore_signal(barrier, inc=1, device_id=p, device_id_type=MESH)

    get_q = fetch(q_in, q_raw, 0)
    get_small = [
        fetch(tk_in, tk, 1), fetch(tv_in, tv, 2), fetch(doc_in, docs_ref, 3),
        fetch(slot_in, slots_ref, 4), fetch(mask_in, mask_ref, 5),
    ]
    get_kv = [fetch(ck_in, k_all.at[0], 6), fetch(cv_in, v_all.at[0], 7)]
    get_w = fetch(w_in, w_all.at[0], 8)

    pl.semaphore_wait(barrier, len(peers))

    def give_k(src, slot, device):
        got = f"k{slot}" if slot in (1, 2, 4, 6) else ("g2" if slot == 3 else "g3")
        send(src, k_all.at[slot], "k", got, device)

    def give_v(src, slot, device):
        got = {1: "v1", 2: "g1", 4: "g1", 3: "g2", 6: "g2"}.get(slot, "g3")
        send(src, v_all.at[slot], "v", got, device)

    give_v(cv_in, 1, to_yx(1))
    for r in (2, 4, 6):
        give_k(ck_in, back_yx(r), to_yx(r))
    give_k(ck_in, 1, to_yx(1))
    for r in (2, 4, 6):
        give_v(cv_in, back_yx(r), to_yx(r))

    get_q.wait()
    i0, i1 = iota((128, 128), 0), iota((128, 128), 1)
    order = (i1 == (i0 % ROWS) * GROUP + i0 // ROWS).astype(BF16)
    q_all[0] = mm(order, q_raw[...]).astype(BF16)
    for d in Z_ORDER:
        slot = ZS.index(NZ - d)
        send(q_all.at[0], q_all.at[slot], "q", f"q{slot // 2}", dev(dz=d))
    for cp in get_small:
        cp.wait()
    mine = jnp.concatenate([tk[...].astype(F32), tv[...].astype(F32)], axis=0).astype(BF16)
    turn_yx[yx] = mine
    turn_all[z, yx] = mine
    for r in YX_ORDER:
        send(turn_yx.at[yx], turn_yx.at[yx], "t", "t", to_yx(r))
    for d in Z_ORDER:
        send(turn_yx.at[yx], turn_all.at[z, yx], "tz", "tz", dev(dz=d))

    docs = docs_ref[...]
    key_token = 16 * z + 8 * (i1 // 16 % 2) + i1 % 8
    by_y = mm(
        jnp.concatenate([docs.astype(F32), jnp.zeros((12, 128), F32)], axis=0).astype(BF16),
        (i0 == key_token).astype(BF16),
    )
    key_doc = jnp.sum(
        jnp.where(iota((16, 128), 0) == iota((16, 128), 1) // 32, by_y, 0.0), axis=0, keepdims=True
    )
    doc_mine = jnp.sum(
        jnp.where(iota((NY, 128), 0) == y, docs, 0), axis=0, keepdims=True
    ).astype(F32)
    right_key = (i1 // 8 % 2 == 0)

    def sight(slot):
        query_token = 16 * around(z, ZS[slot], NZ) + 8 * x + i0 % 8
        query_doc = jnp.sum(jnp.where(i1 == query_token, doc_mine, 0.0), axis=1, keepdims=True)
        see = (
            (128 * (i1 // 32) + key_token <= 128 * y + query_token)
            & (key_doc == query_doc)
            & right_key
        )
        return jnp.where(see, 0.0, NEG)

    diagonal = i0 == i1

    arrived(v_all.at[1], "v1")
    for r in (2, 4, 6):
        give_v(v_all.at[1], back_yx(r + 1), to_yx(r))
    for slot in range(NZ):
        sights[slot] = sight(slot)
    for r in (2, 4, 6):
        arrived(k_all.at[r], f"k{r}")
        give_k(k_all.at[r], r + 1, to_yx(1))
    send(w_in, w_all.at[1], "w", "w", dev(dx=1))

    biases = {}
    for g, i in BLOCKS:
        last = g == 3
        if i == 0:
            if g == 0:
                for cp in get_kv:
                    cp.wait()
                arrived(k_all.at[1], "k1")
            else:
                arrived(k_all.at[pl.ds(0, g + 1)], f"g{g}")
            for j, r in enumerate(KEY_GROUPS[g]):
                v_wide[g, KEYS * j : KEYS * (j + 1), :HEAD] = v_all[r]
            v_wide[g, :, HEAD:] = jnp.ones((2 * KEYS, HEAD), BF16)
            biases[g] = []
            for r in KEY_GROUPS[g]:
                source = (around(y, YX[r][0], NY) * NZ + z) * NX + around(x, YX[r][1], NX)
                for b in range(2):
                    biases[g].append(jnp.where(mask_ref[y, 2 * source + b] == 1, 0.0, NEG))
            if last:
                arrived(turn_yx.at[pl.ds(1, NYX - 1)], "t")
                fresh = turn_yx[...].reshape(128, HEAD)
                fresh_v = mm((i1 == i0 + 8).astype(BF16), fresh).astype(BF16)
                fresh_v = jnp.concatenate([fresh_v, jnp.ones((128, HEAD), BF16)], axis=1)
        if g == 0:
            arrived(q_all.at[pl.ds(2 * i, 2)] if i else q_all.at[1], f"q{i}")
        q = q_all[2 * i : 2 * i + 2].reshape(256, HEAD)
        parts = []
        for j, r in enumerate(KEY_GROUPS[g]):
            s = nt(q, k_all[r])
            parts += [
                s[:, :128] * SCALE + biases[g][2 * j], s[:, 128:] * SCALE + biases[g][2 * j + 1]
            ]
        values = v_wide[g]
        if last:
            parts.append(nt(q, fresh) * SCALE + sights[2 * i : 2 * i + 2].reshape(256, 128))
            values = jnp.concatenate([values, fresh_v], axis=0)
        top = parts[0]
        for p in parts[1:]:
            top = jnp.maximum(top, p)
        top = jnp.broadcast_to(jnp.max(top, axis=1, keepdims=True), (256, 128))
        old = FLOOR if g == 0 else peak[i]
        top = jnp.maximum(top, old)
        p = jnp.concatenate([jnp.exp2(p - top).astype(BF16) for p in parts], axis=1)
        o = mm(p, values)
        if g > 0:
            keep = jnp.exp2(old - top)
            o = o + acc[i] * jnp.concatenate([keep, keep], axis=1)
        if not last:
            acc[i] = o
            peak[i] = top
            continue
        for j in range(2):
            rows = slice(128 * j, 128 * (j + 1))
            of = around(z, ZS[2 * i + j], NZ)
            o_send[:, of] = o[rows, :HEAD].astype(BF16).reshape(NZ, 16, HEAD)
            st_send[pl.ds(of, 1)] = jnp.sum(
                jnp.where(diagonal, top[rows], 0.0), axis=0, keepdims=True
            )
            st_send[pl.ds(NZ + of, 1)] = jnp.sum(
                jnp.where(diagonal, o[rows, HEAD:], 0.0), axis=0, keepdims=True
            )

    for d in Z_ORDER:
        send(st_send, st_recv.at[z], "st", "st", dev(dz=d))
    for d in (4, 3, 5, 2, 6, 1, 7):
        send(o_send.at[around(z, d, NZ)], o_recv.at[z], "rs", "rs", dev(dz=d))
    o_recv[z] = o_send[z]
    st_recv[z] = st_send[...]
    others = pl.ds(1, NZ - 1)
    arrived(turn_all.at[others, 0], "tz")
    for r in YX_ORDER:
        send(turn_all.at[:, yx], turn_all.at[:, yx], "tt", "tt", to_yx(r))
    arrived(st_recv.at[others], "st")
    peaks, totals = st_recv[:, :NZ], st_recv[:, NZ:]
    factor = jnp.exp2(peaks - jnp.max(peaks, axis=0, keepdims=True))
    factor = factor / jnp.sum(factor * totals, axis=0, keepdims=True)
    factors[...] = jnp.concatenate(
        [factor.reshape(NZ * NZ, 128), jnp.zeros((128 - NZ * NZ, 128), F32)], axis=0
    ).T
    factor = factors[pl.ds(pl.multiple_of(16 * z, 16), 16)]
    for at in range(NZ * NZ):
        wide[at] = jnp.broadcast_to(factor[:, at : at + 1], (16, HEAD))

    def attended(half):
        out = []
        for of in (range(NA), range(NA, NZ))[half]:
            num = 0.0
            for j in range(NZ):
                num = num + wide[NZ * j + of] * o_recv[j, of].astype(F32)
            out.append(jnp.concatenate([num[:ROWS], num[ROWS:]], axis=1))
        return jnp.concatenate(out, axis=0).astype(BF16)

    arrived(o_recv.at[others], "rs")
    part_a[0, 0] = attended(0)
    for i in (1, 2, 3):
        send(part_a.at[0, 0], part_a.at[0, back_y(i)], "a1", f"a1_{back_y(i)}", to_y(i))

    def give(slot, i, steps):
        for step in steps:
            dst = (slot - step) % NZ
            if dst != 4 or (step > 0) == (i < NY // 2):
                got = f"a2_{i}" if dst in (2, 6) else ("a2_side" if dst in (1, 7) else "a2_far")
                send(part_a.at[slot, i], part_a.at[dst, i], "a2", got, dev(dz=step))

    give(0, 0, (1, -1, 2, -2))
    part_b[0, 0] = attended(1)
    batch_of = {s: k for k, (lo, hi) in enumerate(Z_BATCHES) for s in range(lo, hi)}
    for d in Z_ORDER:
        slot = ZS.index(NZ - d)
        send(part_b.at[0, 0], part_b.at[slot, 0], "b1", f"b1_{batch_of[slot]}", dev(dz=d))

    def spread(batch):
        lo, hi = Z_BATCHES[batch]
        slots = pl.ds(lo, hi - lo)
        if batch:
            arrived(part_b.at[slots, 0], f"b1_{batch}")
        for i in (1, 2, 3):
            send(part_b.at[slots, 0], part_b.at[slots, back_y(i)], "b2", f"b2_{batch}", to_y(i))

    def spread_arrived(batch):
        lo, hi = Z_BATCHES[batch]
        arrived(part_b.at[pl.ds(lo, hi - lo), pl.ds(1, NY - 1)], f"b2_{batch}")

    def project(part, total, slot, dz, columns):
        at = pl.multiple_of(around(z, dz, NZ) * 256, 256)
        size = part.shape[1] * part.shape[2]
        new = mm(part[slot].reshape(size, 256), w_all[columns, pl.ds(at, 256)])
        total[columns] = new if dz == 0 else total[columns] + new

    def project_a(slots, columns):
        for slot in slots:
            project(part_a, sum_a, slot, slot, columns)

    def project_b(batches, columns):
        for batch in batches:
            for s in range(*Z_BATCHES[batch]):
                project(part_b, sum_b, s, ZS[s], columns)

    spread(0)
    for i in (1, 2, 3):
        arrived(part_a.at[0, i], f"a1_{i}")
        give(0, i, (4, -4, 3, -3, 2, -2, 1, -1) if i == 3 else (1, -1, 2, -2))
        if i == 2:
            spread(1)
    spread(2)
    get_w.wait()
    project_a((0,), 0)
    for i in range(NY):
        arrived(part_a.at[pl.ds(0, 2), i], f"a2_{i}")
        if not (i == 3):
            give(6, i, (1, 2))
            give(2, i, (-1, -2))
        if i < 2:
            spread(3 + i)
    arrived(part_a.at[pl.ds(0, 2)], "a2_side")
    project_a((1, 7, 2, 6), 0)
    for batch in range(3):
        spread_arrived(batch)
        project_b((batch,), 0)

    arrived(w_all.at[1], "w")
    project_a((0, 1, 7, 2, 6), 1)
    project_b((0, 1, 2), 1)

    def rows_of(head, size):
        dy = lax.rem(head + NY - y, NY)
        return pl.ds(pl.multiple_of(size * jnp.where(dy >= 2, 5 - dy, dy), size), size)

    def share(total, sent, got, name, size):
        for columns, d in ((0, 2), (1, 2), (0, 3), (1, 3), (0, 1), (1, 1), (1, 0)):
            slot = NH * columns + d
            back = NH * columns + (NH - d) % NH
            sent[slot] = total[columns, rows_of(around(h, d, NH), size)].astype(BF16)
            send(sent.at[slot], got.at[back], name, name, dev(dx=columns, dh=d))

    def finish(total, got, name, first, size):
        arrived(got.at[pl.ds(1, 2 * NH - 1)], name)
        whole = [total[0, rows_of(h, size)], got[NH].astype(F32)]
        for columns in range(2):
            for d in range(1, NH):
                whole[columns] = whole[columns] + got[NH * columns + d].astype(F32)
            for j in range(size // ROWS):
                at = 16 * (first + j) + 8 * around(x, columns, NX)
                out_ref[pl.ds(pl.multiple_of(at, 8), 8)] = whole[columns][8 * j : 8 * j + 8]
        rows = pl.ds(16 * first, 2 * size)
        outs.append(put(out_ref.at[rows], out_hbm.at[rows], 2 + (first > 0)))

    for batch in (3, 4):
        spread_arrived(batch)
    project_b((3, 4), 0)
    project_b((3, 4), 1)
    share(sum_b, hb_send, hb_recv, "hb", RB)
    arrived(part_a.at[pl.ds(3, 3)], "a2_far")
    project_a((3, 5, 4), 0)
    project_a((3, 5, 4), 1)
    share(sum_a, ha_send, ha_recv, "ha", RA)

    arrived(turn_all.at[:, pl.ds(1, NYX - 1)], "tt")
    col = iota((128, 1024), 1)
    of_piece = 32 * (col // 32 % 4) + 4 * (col // 128) + 2 * (col // 16 % 2) + col // 4 % 2
    slot_of = mm(
        jnp.broadcast_to(slots_ref[...], (16, 128)).astype(BF16),
        (iota((128, 1024), 0) == of_piece).astype(BF16),
    ).astype(jnp.int32)
    row, col = iota((16, 1024), 0), iota((16, 1024), 1)
    chosen = (slot_of == 4 * c + row // 4) & (col % 4 == row % 4)
    every = turn_all[...].reshape(1024, HEAD)
    kind = col // 8 % 2
    ak_ref[...] = mm((chosen & (kind == 0)).astype(BF16), every).astype(BF16)
    av_ref[...] = mm((chosen & (kind == 1)).astype(BF16), every).astype(BF16)
    outs = [put(ak_ref, ak_hbm, 0), put(av_ref, av_hbm, 1)]

    finish(sum_b, hb_recv, "hb", NA, RB)
    left(q_all.at[others], "q")
    left(k_all.at[others], "k")
    left(v_all.at[others], "v")
    left(turn_yx.at[others], "t")
    left(turn_yx.at[others], "tz")
    left(turn_all.at[others], "tt")
    left(st_recv.at[others], "st")
    left(o_recv.at[others], "rs")
    left(part_a.at[0, pl.ds(1, NY - 1)], "a1")
    left(part_b.at[others, 0], "b1")
    left(part_a.at[others], "a2")
    left(part_b.at[:, pl.ds(1, NY - 1)], "b2")
    left(w_all.at[1], "w")
    left(hb_send.at[others], "hb")
    finish(sum_a, ha_recv, "ha", 0, RA)
    left(ha_send.at[others], "ha")
    for cp in outs:
        cp.wait()


def write_out(a_in, b_in, c_in, a_out, b_out, c_out, a_mid, b_mid, c_mid, sems):
    ins = [(a_in, a_mid), (b_in, b_mid), (c_in, c_mid)]
    outs = [(a_mid, a_out), (b_mid, b_out), (c_mid, c_out)]
    ins = [pltpu.make_async_copy(*pair, sems.at[0, i]) for i, pair in enumerate(ins)]
    outs = [pltpu.make_async_copy(*pair, sems.at[1, i]) for i, pair in enumerate(outs)]
    for cp in ins:
        cp.start()
    for i in (1, 2, 0):
        ins[i].wait()
        outs[i].start()
    for cp in outs:
        cp.wait()


def on_device(
    queries, cache_keys, stored_cache_values, turn_keys, turn_values,
    block_mask, doc_ids, slot_ids, out_weight,
):
    anywhere = pl.BlockSpec(memory_space=pl.ANY)
    results = pl.pallas_call(
        kernel,
        out_shape=(
            jax.ShapeDtypeStruct((128, 256), F32),
            jax.ShapeDtypeStruct((16, HEAD), BF16),
            jax.ShapeDtypeStruct((16, HEAD), BF16),
        ),
        in_specs=[anywhere] * 9,
        out_specs=(anywhere,) * 3,
        scratch_shapes=[
            pltpu.VMEM((128, HEAD), BF16),
            pltpu.VMEM((NZ, 128, HEAD), BF16),
            pltpu.VMEM((NYX, KEYS, HEAD), BF16),
            pltpu.VMEM((NYX, KEYS, HEAD), BF16),
            pltpu.VMEM((4, 2 * KEYS, 2 * HEAD), BF16),
            pltpu.VMEM((NX, 2048, 256), BF16),
            pltpu.VMEM((NYX, 16, HEAD), BF16),
            pltpu.VMEM((NZ, NYX, 16, HEAD), BF16),
            pltpu.VMEM((ROWS, HEAD), BF16),
            pltpu.VMEM((ROWS, HEAD), BF16),
            pltpu.VMEM((NY, 128), jnp.int32),
            pltpu.VMEM((1, 128), jnp.int32),
            pltpu.SMEM((NY, 128), jnp.int32),
            pltpu.VMEM((4, 256, 128), F32),
            pltpu.VMEM((4, 256, 256), F32),
            pltpu.VMEM((NZ, NZ, 16, HEAD), BF16),
            pltpu.VMEM((2 * NZ, 128), F32),
            pltpu.VMEM((NZ, NZ, 16, HEAD), BF16),
            pltpu.VMEM((NZ, 2 * NZ, 128), F32),
            pltpu.VMEM((128, 128), F32),
            pltpu.VMEM((NZ * NZ, 16, HEAD), F32),
            pltpu.VMEM((NZ, 128, 128), F32),
            pltpu.VMEM((NZ, NY, RA, 256), BF16),
            pltpu.VMEM((NZ, NY, RB, 256), BF16),
            pltpu.VMEM((NX, NY * RA, 256), F32),
            pltpu.VMEM((NX, NY * RB, 256), F32),
            pltpu.VMEM((2 * NH, RA, 256), BF16),
            pltpu.VMEM((2 * NH, RA, 256), BF16),
            pltpu.VMEM((2 * NH, RB, 256), BF16),
            pltpu.VMEM((2 * NH, RB, 256), BF16),
            pltpu.VMEM((128, 256), F32),
            pltpu.VMEM((16, HEAD), BF16),
            pltpu.VMEM((16, HEAD), BF16),
            pltpu.SemaphoreType.DMA((9,)),
            pltpu.SemaphoreType.DMA((4,)),
            pltpu.SemaphoreType.DMA((len(SENT),)),
            pltpu.SemaphoreType.DMA((len(GOT),)),
        ],
        compiler_params=pltpu.CompilerParams(
            collective_id=0, has_side_effects=True, vmem_limit_bytes=60 * 1024 * 1024
        ),
        name="turn_attention",
    )(
        queries.reshape(128, HEAD),
        cache_keys.reshape(KEYS, HEAD),
        stored_cache_values.reshape(KEYS, HEAD),
        out_weight,
        turn_keys.reshape(ROWS, HEAD),
        turn_values.reshape(ROWS, HEAD),
        doc_ids.reshape(NY, 128),
        slot_ids.reshape(1, 128),
        block_mask,
    )
    layer_out, append_keys, append_values = pl.pallas_call(
        write_out,
        out_shape=tuple(jax.ShapeDtypeStruct(r.shape, r.dtype) for r in results),
        in_specs=[anywhere] * 3,
        out_specs=(anywhere,) * 3,
        scratch_shapes=[pltpu.VMEM(r.shape, r.dtype) for r in results]
        + [pltpu.SemaphoreType.DMA((2, 3))],
        compiler_params=pltpu.CompilerParams(vmem_limit_bytes=60 * 1024 * 1024),
        name="write_out",
    )(*results)
    return (
        layer_out,
        append_keys.reshape(16, 1, HEAD),
        append_values.reshape(16, 1, HEAD),
    )


def solution(mesh):
    placed = (
        P("ctx", "head", None),
        P("ctx", "head", None),
        P("ctx", "head", None),
        P("ctx", "head", None),
        P("ctx", "head", None),
        P(),
        P(),
        P(),
        P("head", "ctx"),
    )
    return jax.shard_map(
        on_device,
        mesh=mesh,
        in_specs=placed,
        out_specs=(P("head", "ctx"), P("ctx", "head", None), P("ctx", "head", None)),
        check_vma=False,
    )
```

```python
import math

import jax
import jax.numpy as jnp
from jax import lax
from jax.experimental import pallas as pl
from jax.experimental.pallas import tpu as pltpu
from jax.sharding import PartitionSpec as P

MESH = pl.DeviceIdType.MESH
F32 = jnp.float32
BF16 = jnp.bfloat16

NY, NZ, NX = 4, 8, 2
NYX = NY * NX
NH = 4
HEAD = 128
KEYS = 256
GROUP = 16
ROWS = 8
NEG = -1e30
FLOOR = -1e29
SCALE = math.log2(math.e) / math.sqrt(HEAD)

YX = [(0, 0), (0, 1), (1, 0), (1, 1), (3, 0), (3, 1), (2, 0), (2, 1)]
YX_ORDER = [1, 2, 4, 3, 5, 6, 7]
YS = [0, 1, 3, 2]
ZS = [0, 1, 7, 2, 6, 3, 5, 4]
Z_ORDER = [1, 7, 2, 6, 3, 5, 4]
Z_BATCHES = [(0, 1), (1, 3), (3, 5), (5, 7), (7, 8)]
NA = 4
RA, RB = NA * ROWS, (NZ - NA) * ROWS
DIRECT = True
GOT = [
    "q0", "q1", "q2", "q3", "v1", "k1", "k2", "k4", "k6", "g1", "g2", "g3", "t", "tz", "tt", "st",
    "rs", "a1_1", "a1_2", "a1_3", "b1_1", "b1_2", "b1_3", "b1_4", "a2_0", "a2_1", "a2_2",
    "a2_3", "a2_side", "a2_far", "b2_0", "b2_1", "b2_2", "b2_3", "b2_4", "ha", "hb", "w",
]
KEY_GROUPS = [(0, 1), (2, 4), (6, 3), (5, 7)]
BLOCKS = [
    (0, 0), (0, 1), (1, 0), (1, 1), (0, 2), (1, 2), (2, 0), (2, 1), (2, 2), (0, 3), (1, 3), (2, 3),
    (3, 0), (3, 1), (3, 2), (3, 3),
]


def nt(a, b):
    return lax.dot_general(a, b, (((1,), (1,)), ((), ())), preferred_element_type=F32)


def mm(a, b):
    return jnp.dot(a, b, preferred_element_type=F32)


def iota(shape, dim):
    return lax.broadcasted_iota(jnp.int32, shape, dim)


def around(i, step, size):
    return lax.rem(i + step % size, size) if step % size else i


def back_yx(r):
    dy, dx = YX[r]
    return YX.index(((NY - dy) % NY, dx))


def kernel(
    q_in, ck_in, cv_in, w_in, tk_in, tv_in, doc_in, slot_in, mask_in,
    out_hbm, ak_hbm, av_hbm,
    q_raw, q_all, k_all, v_all, v_wide, w_all, turn_yx, turn_all, tk, tv, docs_ref, slots_ref, mask_ref,
    peak, acc, o_send, st_send, o_recv, st_recv, factors, wide, sights, part_a, part_b, sum_a, sum_b,
    ha_send, ha_recv, hb_send, hb_recv, out_ref, ak_ref, av_ref,
    sem_in, sem_out, sem_sent, sem_got,
):
    c = lax.axis_index("ctx")
    h = lax.axis_index("head")
    y, z, x = lax.div(c, NZ * NX), lax.rem(lax.div(c, NX), NZ), lax.rem(c, NX)
    yx = y * NX + x

    def dev(dy=0, dz=0, dx=0, dh=0):
        ty, tz, tx = around(y, dy, NY), around(z, dz, NZ), around(x, dx, NX)
        return ((ty * NZ + tz) * NX + tx, around(h, dh, NH))

    def to_y(i):
        return dev(dy=YS[i])

    def back_y(i):
        return YS.index((NY - YS[i]) % NY)

    def to_yx(r):
        return dev(dy=YX[r][0], dx=YX[r][1])

    def send(src, dst, got, device):
        sent = 2 if got == "ha" else (0 if got[0] in "kvgw" else 1)
        pltpu.make_async_remote_copy(
            src_ref=src, dst_ref=dst, send_sem=sem_sent.at[sent],
            recv_sem=sem_got.at[GOT.index(got)], device_id=device, device_id_type=MESH,
        ).start()

    def arrived(ref, got):
        pltpu.make_async_copy(ref, ref, sem_got.at[GOT.index(got)]).wait()

    def left(ref, sent):
        pltpu.make_async_copy(ref, ref, sem_sent.at[sent]).wait()

    def put(src, dst, i):
        copy = pltpu.make_async_copy(src, dst, sem_out.at[i])
        copy.start()
        return copy

    def fetch(src, dst, i):
        copy = pltpu.make_async_copy(src, dst, sem_in.at[i])
        copy.start()
        return copy

    barrier = pltpu.get_barrier_semaphore()
    peers = [dev(dz=d) for d in (4, 3, 5, 2, 6)] + [to_yx(r) for r in (7, 6, 5, 3)]
    peers += [dev(dx=dx, dh=d) for dx in range(NX) for d in range(1, NH)]
    peers += [to_yx(r) for r in (4, 2, 1)] + [dev(dz=d) for d in (1, 7)]
    for p in peers:
        pl.semaphore_signal(barrier, inc=1, device_id=p, device_id_type=MESH)

    get_q = fetch(q_in, q_raw, 0)
    get_small = [
        fetch(tk_in, tk, 1), fetch(tv_in, tv, 2), fetch(doc_in, docs_ref, 3),
        fetch(slot_in, slots_ref, 4), fetch(mask_in, mask_ref, 5),
    ]
    get_kv = [fetch(ck_in, k_all.at[0], 6), fetch(cv_in, v_all.at[0], 7)]
    get_w = fetch(w_in, w_all.at[0], 8)

    pl.semaphore_wait(barrier, len(peers))

    def give_k(src, slot, device):
        got = f"k{slot}" if slot in (1, 2, 4, 6) else ("g2" if slot == 3 else "g3")
        send(src, k_all.at[slot], got, device)

    def give_v(src, slot, device):
        got = {1: "v1", 2: "g1", 4: "g1", 3: "g2", 6: "g2"}.get(slot, "g3")
        send(src, v_all.at[slot], got, device)

    give_v(cv_in, 1, to_yx(1))
    for r in (2, 4, 6):
        give_k(ck_in, back_yx(r), to_yx(r))
    give_k(ck_in, 1, to_yx(1))
    for r in (2, 4, 6):
        give_v(cv_in, back_yx(r), to_yx(r))

    get_q.wait()
    i0, i1 = iota((128, 128), 0), iota((128, 128), 1)
    order = (i1 == (i0 % ROWS) * GROUP + i0 // ROWS).astype(BF16)
    q_all[0] = mm(order, q_raw[...]).astype(BF16)
    for d in Z_ORDER:
        slot = ZS.index(NZ - d)
        send(q_all.at[0], q_all.at[slot], f"q{slot // 2}", dev(dz=d))
    for cp in get_small:
        cp.wait()
    mine = jnp.concatenate([tk[...].astype(F32), tv[...].astype(F32)], axis=0).astype(BF16)
    turn_yx[yx] = mine
    turn_all[z, yx] = mine
    for r in YX_ORDER:
        send(turn_yx.at[yx], turn_yx.at[yx], "t", to_yx(r))
    for d in Z_ORDER:
        send(turn_yx.at[yx], turn_all.at[z, yx], "tz", dev(dz=d))

    docs = docs_ref[...]
    key_token = 16 * z + 8 * (i1 // 16 % 2) + i1 % 8
    by_y = mm(
        jnp.concatenate([docs.astype(F32), jnp.zeros((12, 128), F32)], axis=0).astype(BF16),
        (i0 == key_token).astype(BF16),
    )
    key_doc = jnp.sum(
        jnp.where(iota((16, 128), 0) == iota((16, 128), 1) // 32, by_y, 0.0), axis=0, keepdims=True
    )
    doc_mine = jnp.sum(
        jnp.where(iota((NY, 128), 0) == y, docs, 0), axis=0, keepdims=True
    ).astype(F32)
    right_key = (i1 // 8 % 2 == 0)

    def sight(slot):
        query_token = 16 * around(z, ZS[slot], NZ) + 8 * x + i0 % 8
        query_doc = jnp.sum(jnp.where(i1 == query_token, doc_mine, 0.0), axis=1, keepdims=True)
        see = (
            (128 * (i1 // 32) + key_token <= 128 * y + query_token)
            & (key_doc == query_doc)
            & right_key
        )
        return jnp.where(see, 0.0, NEG)

    diagonal = i0 == i1

    arrived(v_all.at[1], "v1")
    for r in (2, 4, 6):
        give_v(v_all.at[1], back_yx(r + 1), to_yx(r))
    for slot in range(NZ):
        sights[slot] = sight(slot)
    for r in (2, 4, 6):
        arrived(k_all.at[r], f"k{r}")
        give_k(k_all.at[r], r + 1, to_yx(1))
    send(w_in, w_all.at[1], "w", dev(dx=1))

    biases = {}
    for g, i in BLOCKS:
        last = g == 3
        if i == 0:
            if g == 0:
                for cp in get_kv:
                    cp.wait()
                arrived(k_all.at[1], "k1")
            else:
                arrived(k_all.at[pl.ds(0, g + 1)], f"g{g}")
            for j, r in enumerate(KEY_GROUPS[g]):
                v_wide[g, KEYS * j : KEYS * (j + 1), :HEAD] = v_all[r]
            v_wide[g, :, HEAD:] = jnp.ones((2 * KEYS, HEAD), BF16)
            biases[g] = []
            for r in KEY_GROUPS[g]:
                source = (around(y, YX[r][0], NY) * NZ + z) * NX + around(x, YX[r][1], NX)
                for b in range(2):
                    biases[g].append(jnp.where(mask_ref[y, 2 * source + b] == 1, 0.0, NEG))
            if last:
                arrived(turn_yx.at[pl.ds(1, NYX - 1)], "t")
                fresh = turn_yx[...].reshape(128, HEAD)
                fresh_v = mm((i1 == i0 + 8).astype(BF16), fresh).astype(BF16)
                fresh_v = jnp.concatenate([fresh_v, jnp.ones((128, HEAD), BF16)], axis=1)
        if g == 0:
            arrived(q_all.at[pl.ds(2 * i, 2)] if i else q_all.at[1], f"q{i}")
        q = q_all[2 * i : 2 * i + 2].reshape(256, HEAD)
        parts = []
        for j, r in enumerate(KEY_GROUPS[g]):
            s = nt(q, k_all[r])
            parts += [
                s[:, :128] * SCALE + biases[g][2 * j], s[:, 128:] * SCALE + biases[g][2 * j + 1]
            ]
        values = v_wide[g]
        if last:
            parts.append(nt(q, fresh) * SCALE + sights[2 * i : 2 * i + 2].reshape(256, 128))
            values = jnp.concatenate([values, fresh_v], axis=0)
        top = parts[0]
        for p in parts[1:]:
            top = jnp.maximum(top, p)
        top = jnp.broadcast_to(jnp.max(top, axis=1, keepdims=True), (256, 128))
        old = FLOOR if g == 0 else peak[i]
        top = jnp.maximum(top, old)
        p = jnp.concatenate([jnp.exp2(p - top).astype(BF16) for p in parts], axis=1)
        o = mm(p, values)
        if g > 0:
            keep = jnp.exp2(old - top)
            o = o + acc[i] * jnp.concatenate([keep, keep], axis=1)
        if not last:
            acc[i] = o
            peak[i] = top
            continue
        for j in range(2):
            rows = slice(128 * j, 128 * (j + 1))
            of = around(z, ZS[2 * i + j], NZ)
            o_send[:, of] = o[rows, :HEAD].astype(BF16).reshape(NZ, 16, HEAD)
            st_send[pl.ds(of, 1)] = jnp.sum(
                jnp.where(diagonal, top[rows], 0.0), axis=0, keepdims=True
            )
            st_send[pl.ds(NZ + of, 1)] = jnp.sum(
                jnp.where(diagonal, o[rows, HEAD:], 0.0), axis=0, keepdims=True
            )

    for d in Z_ORDER:
        send(st_send, st_recv.at[z], "st", dev(dz=d))
    for d in (4, 3, 5, 2, 6, 1, 7):
        send(o_send.at[around(z, d, NZ)], o_recv.at[z], "rs", dev(dz=d))
    o_recv[z] = o_send[z]
    st_recv[z] = st_send[...]
    others = pl.ds(1, NZ - 1)
    arrived(turn_all.at[others, 0], "tz")
    for r in YX_ORDER:
        send(turn_all.at[:, yx], turn_all.at[:, yx], "tt", to_yx(r))
    arrived(st_recv.at[others], "st")
    peaks, totals = st_recv[:, :NZ], st_recv[:, NZ:]
    factor = jnp.exp2(peaks - jnp.max(peaks, axis=0, keepdims=True))
    factor = factor / jnp.sum(factor * totals, axis=0, keepdims=True)
    factors[...] = jnp.concatenate(
        [factor.reshape(NZ * NZ, 128), jnp.zeros((128 - NZ * NZ, 128), F32)], axis=0
    ).T
    factor = factors[pl.ds(pl.multiple_of(16 * z, 16), 16)]
    for at in range(NZ * NZ):
        wide[at] = jnp.broadcast_to(factor[:, at : at + 1], (16, HEAD))

    def attended(half):
        out = []
        for of in (range(NA), range(NA, NZ))[half]:
            num = 0.0
            for j in range(NZ):
                num = num + wide[NZ * j + of] * o_recv[j, of].astype(F32)
            out.append(jnp.concatenate([num[:ROWS], num[ROWS:]], axis=1))
        return jnp.concatenate(out, axis=0).astype(BF16)

    arrived(o_recv.at[others], "rs")
    part_a[0, 0] = attended(0)
    for i in (1, 2, 3):
        send(part_a.at[0, 0], part_a.at[0, back_y(i)], f"a1_{back_y(i)}", to_y(i))

    def give(slot, i, steps):
        for step in steps:
            dst = (slot - step) % NZ
            if dst != 4 or (step > 0) == (i < NY // 2):
                got = f"a2_{i}" if dst in (2, 6) else ("a2_side" if dst in (1, 7) else "a2_far")
                send(part_a.at[slot, i], part_a.at[dst, i], got, dev(dz=step))

    give(0, 0, (1, -1, 2, -2))
    part_b[0, 0] = attended(1)
    batch_of = {s: k for k, (lo, hi) in enumerate(Z_BATCHES) for s in range(lo, hi)}
    for d in Z_ORDER:
        slot = ZS.index(NZ - d)
        send(part_b.at[0, 0], part_b.at[slot, 0], f"b1_{batch_of[slot]}", dev(dz=d))

    def spread(batch):
        lo, hi = Z_BATCHES[batch]
        slots = pl.ds(lo, hi - lo)
        if batch:
            arrived(part_b.at[slots, 0], f"b1_{batch}")
        for i in (1, 2, 3):
            send(part_b.at[slots, 0], part_b.at[slots, back_y(i)], f"b2_{batch}", to_y(i))

    def spread_arrived(batch):
        lo, hi = Z_BATCHES[batch]
        arrived(part_b.at[pl.ds(lo, hi - lo), pl.ds(1, NY - 1)], f"b2_{batch}")

    def project(part, total, slot, dz, columns):
        at = pl.multiple_of(around(z, dz, NZ) * 256, 256)
        size = part.shape[1] * part.shape[2]
        new = mm(part[slot].reshape(size, 256), w_all[columns, pl.ds(at, 256)])
        total[columns] = new if dz == 0 else total[columns] + new

    def project_a(slots, columns):
        for slot in slots:
            project(part_a, sum_a, slot, slot, columns)

    def project_b(batches, columns):
        for batch in batches:
            for s in range(*Z_BATCHES[batch]):
                project(part_b, sum_b, s, ZS[s], columns)

    spread(0)
    for i in (1, 2, 3):
        arrived(part_a.at[0, i], f"a1_{i}")
        give(0, i, (1, -1, 2, -2))
        if i == 2:
            spread(1)
    spread(2)
    get_w.wait()
    project_a((0,), 0)
    for i in range(NY):
        arrived(part_a.at[pl.ds(0, 2), i], f"a2_{i}")
        give(6, i, (1, 2))
        give(2, i, (-1, -2))
        if i < 2:
            spread(3 + i)
    arrived(part_a.at[pl.ds(0, 2)], "a2_side")
    project_a((1, 7, 2, 6), 0)
    for batch in range(3):
        spread_arrived(batch)
        project_b((batch,), 0)

    arrived(w_all.at[1], "w")
    project_a((0, 1, 7, 2, 6), 1)
    project_b((0, 1, 2), 1)

    def rows_of(head, size):
        dy = lax.rem(head + NY - y, NY)
        return pl.ds(pl.multiple_of(size * jnp.where(dy >= 2, 5 - dy, dy), size), size)

    def share(total, sent, got, name, size):
        for columns, d in ((0, 2), (1, 2), (0, 3), (1, 3), (0, 1), (1, 1), (1, 0)):
            slot = NH * columns + d
            back = NH * columns + (NH - d) % NH
            sent[slot] = total[columns, rows_of(around(h, d, NH), size)].astype(BF16)
            send(sent.at[slot], got.at[back], name, dev(dx=columns, dh=d))

    def finish(total, got, name, first, size):
        arrived(got.at[pl.ds(1, 2 * NH - 1)], name)
        whole = [total[0, rows_of(h, size)], got[NH].astype(F32)]
        for columns in range(2):
            for d in range(1, NH):
                whole[columns] = whole[columns] + got[NH * columns + d].astype(F32)
            for j in range(size // ROWS):
                at = 16 * (first + j) + 8 * around(x, columns, NX)
                out_ref[pl.ds(pl.multiple_of(at, 8), 8)] = whole[columns][8 * j : 8 * j + 8]
        rows = pl.ds(16 * first, 2 * size)
        outs.append(put(out_ref.at[rows], out_hbm.at[rows], 2 + (first > 0)))

    for batch in (3, 4):
        spread_arrived(batch)
    project_b((3, 4), 0)
    project_b((3, 4), 1)
    share(sum_b, hb_send, hb_recv, "hb", RB)
    arrived(part_a.at[pl.ds(3, 3)], "a2_far")
    project_a((3, 5, 4), 0)
    project_a((3, 5, 4), 1)
    share(sum_a, ha_send, ha_recv, "ha", RA)

    arrived(turn_all.at[:, pl.ds(1, NYX - 1)], "tt")
    col = iota((128, 1024), 1)
    of_piece = 32 * (col // 32 % 4) + 4 * (col // 128) + 2 * (col // 16 % 2) + col // 4 % 2
    slot_of = mm(
        jnp.broadcast_to(slots_ref[...], (16, 128)).astype(BF16),
        (iota((128, 1024), 0) == of_piece).astype(BF16),
    ).astype(jnp.int32)
    row, col = iota((16, 1024), 0), iota((16, 1024), 1)
    chosen = (slot_of == 4 * c + row // 4) & (col % 4 == row % 4)
    every = turn_all[...].reshape(1024, HEAD)
    kind = col // 8 % 2
    ak_ref[...] = mm((chosen & (kind == 0)).astype(BF16), every).astype(BF16)
    av_ref[...] = mm((chosen & (kind == 1)).astype(BF16), every).astype(BF16)
    outs = [put(ak_ref, ak_hbm, 0), put(av_ref, av_hbm, 1)]

    finish(sum_b, hb_recv, "hb", NA, RB)
    left(w_all.at[:, pl.ds(0, 1024 + 2 * 448)], 0)
    left(w_all.at[:, pl.ds(0, 2 * 224 + 2 * 28 + 56 + 224 + 48 + 112 + 448 + 384 + 112)], 1)
    finish(sum_a, ha_recv, "ha", 0, RA)
    left(ha_send.at[others], 2)
    for cp in outs:
        cp.wait()


def write_out(a_in, b_in, c_in, a_out, b_out, c_out, a_mid, b_mid, c_mid, sems):
    ins = [(a_in, a_mid), (b_in, b_mid), (c_in, c_mid)]
    outs = [(a_mid, a_out), (b_mid, b_out), (c_mid, c_out)]
    ins = [pltpu.make_async_copy(*pair, sems.at[0, i]) for i, pair in enumerate(ins)]
    outs = [pltpu.make_async_copy(*pair, sems.at[1, i]) for i, pair in enumerate(outs)]
    for cp in ins:
        cp.start()
    for i in (1, 2, 0):
        ins[i].wait()
        outs[i].start()
    for cp in outs:
        cp.wait()


def on_device(
    queries, cache_keys, stored_cache_values, turn_keys, turn_values,
    block_mask, doc_ids, slot_ids, out_weight,
):
    anywhere = pl.BlockSpec(memory_space=pl.ANY)
    results = pl.pallas_call(
        kernel,
        out_shape=(
            jax.ShapeDtypeStruct((128, 256), F32),
            jax.ShapeDtypeStruct((16, HEAD), BF16),
            jax.ShapeDtypeStruct((16, HEAD), BF16),
        ),
        in_specs=[anywhere] * 9,
        out_specs=(anywhere,) * 3,
        scratch_shapes=[
            pltpu.VMEM((128, HEAD), BF16),
            pltpu.VMEM((NZ, 128, HEAD), BF16),
            pltpu.VMEM((NYX, KEYS, HEAD), BF16),
            pltpu.VMEM((NYX, KEYS, HEAD), BF16),
            pltpu.VMEM((4, 2 * KEYS, 2 * HEAD), BF16),
            pltpu.VMEM((NX, 2048, 256), BF16),
            pltpu.VMEM((NYX, 16, HEAD), BF16),
            pltpu.VMEM((NZ, NYX, 16, HEAD), BF16),
            pltpu.VMEM((ROWS, HEAD), BF16),
            pltpu.VMEM((ROWS, HEAD), BF16),
            pltpu.VMEM((NY, 128), jnp.int32),
            pltpu.VMEM((1, 128), jnp.int32),
            pltpu.SMEM((NY, 128), jnp.int32),
            pltpu.VMEM((4, 256, 128), F32),
            pltpu.VMEM((4, 256, 256), F32),
            pltpu.VMEM((NZ, NZ, 16, HEAD), BF16),
            pltpu.VMEM((2 * NZ, 128), F32),
            pltpu.VMEM((NZ, NZ, 16, HEAD), BF16),
            pltpu.VMEM((NZ, 2 * NZ, 128), F32),
            pltpu.VMEM((128, 128), F32),
            pltpu.VMEM((NZ * NZ, 16, HEAD), F32),
            pltpu.VMEM((NZ, 128, 128), F32),
            pltpu.VMEM((NZ, NY, RA, 256), BF16),
            pltpu.VMEM((NZ, NY, RB, 256), BF16),
            pltpu.VMEM((NX, NY * RA, 256), F32),
            pltpu.VMEM((NX, NY * RB, 256), F32),
            pltpu.VMEM((2 * NH, RA, 256), BF16),
            pltpu.VMEM((2 * NH, RA, 256), BF16),
            pltpu.VMEM((2 * NH, RB, 256), BF16),
            pltpu.VMEM((2 * NH, RB, 256), BF16),
            pltpu.VMEM((128, 256), F32),
            pltpu.VMEM((16, HEAD), BF16),
            pltpu.VMEM((16, HEAD), BF16),
            pltpu.SemaphoreType.DMA((9,)),
            pltpu.SemaphoreType.DMA((4,)),
            pltpu.SemaphoreType.DMA((3,)),
            pltpu.SemaphoreType.DMA((len(GOT),)),
        ],
        compiler_params=pltpu.CompilerParams(
            collective_id=0, has_side_effects=True, vmem_limit_bytes=60 * 1024 * 1024
        ),
        name="turn_attention",
    )(
        queries.reshape(128, HEAD),
        cache_keys.reshape(KEYS, HEAD),
        stored_cache_values.reshape(KEYS, HEAD),
        out_weight,
        turn_keys.reshape(ROWS, HEAD),
        turn_values.reshape(ROWS, HEAD),
        doc_ids.reshape(NY, 128),
        slot_ids.reshape(1, 128),
        block_mask,
    )
    layer_out, append_keys, append_values = pl.pallas_call(
        write_out,
        out_shape=tuple(jax.ShapeDtypeStruct(r.shape, r.dtype) for r in results),
        in_specs=[anywhere] * 3,
        out_specs=(anywhere,) * 3,
        scratch_shapes=[pltpu.VMEM(r.shape, r.dtype) for r in results]
        + [pltpu.SemaphoreType.DMA((2, 3))],
        compiler_params=pltpu.CompilerParams(vmem_limit_bytes=60 * 1024 * 1024),
        name="write_out",
    )(*results)
    return (
        layer_out,
        append_keys.reshape(16, 1, HEAD),
        append_values.reshape(16, 1, HEAD),
    )


def solution(mesh):
    placed = (
        P("ctx", "head", None),
        P("ctx", "head", None),
        P("ctx", "head", None),
        P("ctx", "head", None),
        P("ctx", "head", None),
        P(),
        P(),
        P(),
        P("head", "ctx"),
    )
    return jax.shard_map(
        on_device,
        mesh=mesh,
        in_specs=placed,
        out_specs=(P("head", "ctx"), P("ctx", "head", None), P("ctx", "head", None)),
        check_vma=False,
    )
```
